32 devices in a mesh: subj: 4 (over x, core), space: 8 (over z, y).
Axes of the slice: x: 2, y: 2, z: 4, core: 2. Of those that a mesh axis runs over, the one named last changes fastest.
Arguments:
- images: bfloat16 [8, 512, 16, 128], P('subj', 'space'), may hold values from -6 to 6
- velocity: float32 [3, 8, 512, 16, 128], P(None, 'subj', 'space'), may hold values from -4 to 4
- weights: bfloat16 [3, 8, 512, 16, 128], P(None, 'subj', 'space'), may hold values from 0 to 1
- template: float32 [512, 16, 128], P('space', 'subj'), may hold values from -6 to 6
- owners: int32 [8, 512, 1], P('subj', 'space'), may hold values from 0 to 7; in each aligned block of 64 rows (0 to 63, 64 to 127, ..., all dimensions but the last counted through in order) at most 16 rows name the same one
- local_rows: int32 [8, 512], P('subj', 'space'), may hold values from 0 to 63
- tile_counts: int32 [8, 8], P('subj', 'space'), may hold values from 32 to 64
Outputs:
- new_velocity: float32 [3, 8, 512, 16, 128], P(None, 'subj', 'space')
- new_template: float32 [512, 16, 128], P('space', 'subj')
The draws below stay inside these ranges and needn't reach their ends.
Inputs may be any that keep to these rules, and one draw needn't show every extreme that they name: `owners`: for each subject and each aligned block of 64 tiles, no value appears more than 16 times, and some value appears exactly 16 times.
All inputs are finite; a program needn't handle non-finite values.
Results may differ from the reference program's by a relative error of at most 0.0006.
Values may be sent and summed in bfloat16 or wider, within the bound.
No kernel may reach another device: no remote copies, remote signals or barrier semaphores. Data moves between devices by JAX's collectives and lax.ppermute only.
A program may use at most 64 MiB of HBM per device.

```python
import math
import jax
import jax.numpy as jnp
import numpy as np
from jax import lax

BX = 4
BY = 4
BZ = 128
PLANE = 16
SUBJ = 8
ROWS_DEV = 64
ROWS = 512
CAP = 16
ITERS = 2
N_SPACE = 8


def place_ends(values, rng, least, high):
    longest = values.shape.index(max(values.shape))
    spots = []
    for shift in (0, 1):
        where = [jax.random.randint(jax.random.fold_in(rng, axis), (), 0, length) for axis, length in enumerate(values.shape)]
        where[longest] = (where[longest] + shift) % values.shape[longest]
        spots.append(tuple(where))
    return values.at[spots[0]].set(least).at[spots[1]].set(high)


def levels(key, dims, shards, low, largest):
    gain = 1.0
    for dim, blocks in shards:
        draws = jax.random.uniform(jax.random.fold_in(jax.random.fold_in(key, 6), dim), (blocks,), jnp.float32, low / len(shards), largest / len(shards))
        gain = gain * jnp.repeat(jnp.exp(draws), dims[dim] // blocks).reshape((-1,) + (1,) * (len(dims) - 1 - dim))
    return gain


def shared_out(own_key, own, number, rows, count, top, most, slope):
    sequence = jax.random.permutation(own_key, count)
    packed, common = load_shares(count, rows * top, most, slope, True), load_shares(count, rows * top, most, slope, False)
    places = jnp.arange(count)

    def named(sizes, rotation):
        used = int((sizes > 0).sum())
        fixed = max(1, used // 4)
        passed = fixed + (places - fixed + rotation * (used - fixed)) % max(1, count - fixed)
        return jnp.zeros((count,), jnp.int32).at[sequence[jnp.where(places < fixed, places, passed)]].set(jnp.asarray(sizes, jnp.int32))

    sizes = jnp.where(number % 4 == 0, named(packed, number // 4), named(common, number - number // 4 - 1))
    mixed = jax.random.permutation(jax.random.fold_in(own, 3), count)
    giver, taker = mixed[0:count // 2 * 2:2], mixed[1:count // 2 * 2:2]
    room = jnp.minimum(sizes[giver] - 1, most - sizes[taker]) // 2
    room = jnp.where((giver == sequence[0]) | (taker == sequence[0]) | (sizes[taker] == 0), 0, jnp.maximum(room, 0))
    passed = jax.random.randint(jax.random.fold_in(own, 4), (count // 2,), 0, 1 << 20) % (room + 1)
    sizes = sizes.at[giver].add(-passed).at[taker].add(passed)
    labels = jnp.searchsorted(jnp.cumsum(sizes), jnp.arange(rows * top), side="right").astype(jnp.int32)
    grid = labels.reshape(top, rows).T
    grid = grid[jax.random.permutation(jax.random.fold_in(own, 1), rows)]
    rotation = jax.random.randint(jax.random.fold_in(own, 2), (rows, 1), 0, top)
    return jnp.take_along_axis(grid, (jnp.arange(top)[None, :] + rotation) % top, axis=1)


def load_shares(count, total, bound, lean, full):
    weights = [(1 << 20) // math.isqrt(standing ** lean) + 1 for standing in range(1, count + 1)]
    largest = bound if full else min(bound, max(-(-total // count), total * weights[0] // sum(weights)))
    least = 1 if total - largest >= count - 1 else 0
    given, spare = [largest] + [least] * (count - 1), total - largest - least * (count - 1)
    while spare > 0:
        movable = [i for i in range(1, count) if given[i] < largest] or [i for i in range(1, count) if given[i] < bound]
        whole, left = sum([weights[i] for i in movable]), spare
        for i in movable:
            more = min(bound - given[i], max(1, left * weights[i] // whole), spare)
            given[i] = given[i] + more
            spare = spare - more
    return np.array(given)


def bell_draw(own_key, dims, scale, limit, split=(), kind=jnp.bfloat16):
    gain = levels(own_key, dims, split, -0.22, 0.18) if split else 1.0
    values = jax.random.normal(own_key, dims, jnp.float32) * scale * gain
    return jnp.minimum(jnp.maximum(values, -limit), limit).astype(kind)


def setup_inputs(seed: int = 0) -> dict:
    key_list = jax.random.split(jax.random.key(seed), 8)
    images = bell_draw(key_list[0], (SUBJ, ROWS, PLANE, BZ), 1.0, 6.0, ((0, 4), (1, 8)))
    velocity = bell_draw(key_list[1], (3, SUBJ, ROWS, PLANE, BZ), 0.3, 4.0, ((1, 4), (2, 8)), jnp.float32)
    weights = jnp.clip(1.0 * jax.random.uniform(key_list[2], (3, SUBJ, ROWS, PLANE, BZ), jnp.float32) ** levels(key_list[2], (3, SUBJ, ROWS, PLANE, BZ), ((1, 4), (2, 8)), -0.2, 0.2), 0.0, 1.0).astype(jnp.bfloat16)
    template = bell_draw(key_list[3], (ROWS, PLANE, BZ), 1.0, 6.0, ((0, 8), (1, 4)), jnp.float32)
    owners_keys = jax.random.split(jax.random.fold_in(key_list[4], 1), SUBJ * ROWS // ROWS_DEV)
    owners_turns = jax.random.permutation(jax.random.fold_in(key_list[4], 3), SUBJ * ROWS // ROWS_DEV)
    owners = jax.vmap(lambda own, number: shared_out(jax.random.fold_in(key_list[4], 2), own, number, ROWS_DEV, N_SPACE, 1, CAP, 1))(owners_keys, owners_turns).reshape((SUBJ, ROWS, 1))
    local_rows = place_ends(jax.random.randint(key_list[5], (SUBJ, ROWS), 0, ROWS_DEV), jax.random.fold_in(key_list[5], 1), 0, ROWS_DEV - 1).astype(jnp.int32)
    tile_counts = place_ends(jax.random.randint(key_list[6], (SUBJ, N_SPACE), ROWS_DEV // 2, ROWS_DEV + 1), jax.random.fold_in(key_list[6], 1), ROWS_DEV // 2, ROWS_DEV).astype(jnp.int32)
    return {"images": images, "velocity": velocity, "weights": weights, "template": template, "owners": owners, "local_rows": local_rows, "tile_counts": tile_counts}


ridge = 0.25


def shift_up(field, axis):
    body_part = lax.slice_in_dim(field, 1, field.shape[axis], axis=axis)
    edge = jnp.zeros_like(lax.slice_in_dim(field, 0, 1, axis=axis))
    return jnp.concatenate([body_part, edge], axis)


def shift_down(field, axis):
    body_part = lax.slice_in_dim(field, 0, field.shape[axis] - 1, axis=axis)
    edge = jnp.zeros_like(lax.slice_in_dim(field, 0, 1, axis=axis))
    return jnp.concatenate([edge, body_part], axis)


def trilinear(brick, frac_x, frac_y, frac_z):
    depth = brick.ndim
    total = jnp.zeros_like(brick)
    for offset_x in (0, 1):
        moved_x = brick if offset_x == 0 else shift_up(brick, depth - 3)
        weight_x = (1.0 - frac_x) if offset_x == 0 else frac_x
        for offset_y in (0, 1):
            moved = moved_x if offset_y == 0 else shift_up(moved_x, depth - 2)
            weight_y = (1.0 - frac_y) if offset_y == 0 else frac_y
            along_z = (1.0 - frac_z) * moved + frac_z * shift_up(moved, depth - 1)
            total = total + weight_x * weight_y * along_z
    return total


def gradients(field):
    depth = field.ndim
    return jnp.stack([0.5 * (shift_up(field, depth - 3 + offset) - shift_down(field, depth - 3 + offset)) for offset in range(3)])


def smooth_z(field):
    depth = field.ndim
    return 0.25 * shift_down(field, depth - 1) + 0.5 * field + 0.25 * shift_up(field, depth - 1)


def predict(warped, grads, field):
    return warped + (grads[0] * field[0] + grads[1] * field[1]) + grads[2] * field[2]


def reference(images, velocity, weights, template, owners, local_rows, tile_counts):
    rows = ROWS_DEV * N_SPACE
    source = (owners[:, :, 0] * ROWS_DEV + local_rows).astype(jnp.int32)
    tiles = jnp.arange(rows, dtype=jnp.int32)
    counts = jnp.take(tile_counts, tiles // ROWS_DEV, axis=1)
    first = counts // 2
    position = (tiles % ROWS_DEV)[None, :]
    live = ((position < first) | (position >= ROWS_DEV - (counts - first))).astype(jnp.float32)
    fractions = jnp.moveaxis(weights, 1, 0)

    def warp_subject(items):
        image, src, alive, frac = items
        brick = image[src].astype(jnp.float32).reshape(rows, BX, BY, BZ)
        frac = frac.astype(jnp.float32).reshape(3, rows, BX, BY, BZ)
        warped = trilinear(brick, frac[0], frac[1], frac[2]) * alive[:, None, None, None]
        return warped, gradients(warped)

    warped, grads = lax.map(warp_subject, (images, source, live, fractions))
    grads = jnp.moveaxis(grads, 1, 0)
    field = velocity.reshape(3, SUBJ, rows, BX, BY, BZ)
    current = template.reshape(rows, BX, BY, BZ)
    for step in range(ITERS):
        predicted = predict(warped, grads, field)
        ratio = (predicted - current[None]) / (grads[0] * grads[0] + grads[1] * grads[1] + grads[2] * grads[2] + ridge)
        update = grads * ratio[None]
        rowwise = 0.25 * shift_down(update, 2) + 0.5 * update + 0.25 * shift_up(update, 2)
        field = field - smooth_z(rowwise)
        current = jnp.sum(predict(warped, grads, field), axis=0) / SUBJ
    return field.reshape(3, SUBJ, rows, PLANE, BZ), current.reshape(rows, PLANE, BZ)
```

```python
import functools

import jax
import jax.numpy as jnp
from jax import lax
from jax.experimental import pallas as pl
from jax.experimental.pallas import tpu as pltpu
from jax.sharding import PartitionSpec as P

BY = 4
ITERS = 2
RIDGE = 0.25
LANES = 128
BLOCK = 16
LIMIT = 48 * 1024 * 1024


def params():
    return pltpu.CompilerParams(vmem_limit_bytes=LIMIT)


VMEM = pl.BlockSpec(memory_space=pltpu.VMEM)
SMEM = pl.BlockSpec(memory_space=pltpu.SMEM)
ANY = pl.BlockSpec(memory_space=pl.ANY)


def plan_kernel(cap, counts_ref, owners_ref, rows_ref, request_ref, slots_ref):
    subj_dev, rows = rows_ref.shape
    spaces = request_ref.shape[0]
    t = lax.broadcasted_iota(jnp.int32, (rows, rows), 0)
    u = lax.broadcasted_iota(jnp.int32, (rows, rows), 1)
    eye = t == u
    lane = lax.broadcasted_iota(jnp.int32, (rows, LANES), 1)
    sub = lax.broadcasted_iota(jnp.int32, (spaces, LANES), 0)
    zero = jnp.zeros((rows, rows), jnp.int32)
    request = jnp.zeros((spaces, LANES), jnp.int32)
    earlier_subjects = []
    for s in range(subj_dev):
        count = counts_ref[s, 0]
        first = lax.shift_right_logical(count, 1)
        owner_t = jnp.broadcast_to(owners_ref[s], (rows, rows))
        owner_u = jnp.broadcast_to(
            jnp.sum(jnp.where(eye, owner_t, zero), axis=0, keepdims=True), (rows, rows)
        )
        row_u = jnp.broadcast_to(rows_ref[s : s + 1, :], (rows, rows))
        row_t = jnp.broadcast_to(
            jnp.sum(jnp.where(eye, row_u, zero), axis=1, keepdims=True), (rows, rows)
        )
        last = rows - (count - first)
        alive_t = (t < first) | (t >= last)
        alive_u = (u < first) | (u >= last)
        same_owner = owner_t == owner_u
        same = same_owner & (row_t == row_u)
        dup_u = jnp.sum(jnp.where(same & alive_t & (t < u), 1, 0), axis=0, keepdims=True)
        dup_t = jnp.sum(jnp.where(same & alive_u & (u < t), 1, 0), axis=1, keepdims=True)
        first_u = alive_u & jnp.broadcast_to(dup_u == 0, (rows, rows))
        first_t = alive_t & jnp.broadcast_to(dup_t == 0, (rows, rows))
        place = jnp.sum(
            jnp.where(same_owner & first_u & (u < t), 1, 0), axis=1, keepdims=True
        )
        for owner_v, first_v in earlier_subjects:
            place = place + jnp.sum(
                jnp.where((owner_t == owner_v) & first_v, 1, 0), axis=1, keepdims=True
            )
        earlier_subjects.append((owner_u, first_u))
        slot_t = owner_t * cap + place
        slots_ref[s : s + 1, :] = jnp.sum(
            jnp.where(same & first_t & alive_u, slot_t, zero), axis=0, keepdims=True
        )
        wide_first = jnp.broadcast_to(first_t[:, :1], (rows, LANES))
        wide_owner = jnp.broadcast_to(owner_t[:, :1], (rows, LANES))
        wide_place = jnp.broadcast_to(place, (rows, LANES))
        wide_row = jnp.broadcast_to(row_t[:, :1], (rows, LANES)) + s * rows
        hit = jnp.where(wide_first & (wide_place == lane), wide_row, 0)
        for o in range(spaces):
            line = jnp.sum(jnp.where(wide_owner == o, hit, 0), axis=0, keepdims=True)
            request = request + jnp.where(sub == o, line, 0)
    request_ref[...] = request


def plan(counts, owners, local_rows, cap, spaces):
    subj_dev, rows = local_rows.shape
    return pl.pallas_call(
        functools.partial(plan_kernel, cap),
        out_shape=(
            jax.ShapeDtypeStruct((spaces, LANES), jnp.int32),
            jax.ShapeDtypeStruct((subj_dev, rows), jnp.int32),
        ),
        in_specs=[SMEM, VMEM, VMEM],
        out_specs=(VMEM, VMEM),
        compiler_params=params(),
        name="plan",
    )(counts, owners, local_rows)


def pick_kernel(me_ref, wanted_ref, images_ref, *outs):
    me = me_ref[0]
    for k, out in enumerate(outs):
        target = lax.bitwise_xor(me, k)
        for c in range(out.shape[0]):
            out[c] = images_ref[wanted_ref[target, c]]


def pick(me, wanted, images, cap):
    spaces = wanted.shape[0]
    one = jax.ShapeDtypeStruct((cap,) + images.shape[1:], images.dtype)
    return pl.pallas_call(
        pick_kernel,
        out_shape=[one] * spaces,
        in_specs=[SMEM, SMEM, VMEM],
        out_specs=[VMEM] * spaces,
        compiler_params=params(),
        name="pick",
    )(me, wanted, images)


def up_x(v):
    return pltpu.roll(v, v.shape[0] - BY, 0)


def up_y(v):
    return pltpu.roll(v, v.shape[0] - 1, 0)


def up_z(v):
    return pltpu.roll(v, v.shape[1] - 1, 1)


def down_x(v):
    return pltpu.roll(v, BY, 0)


def down_y(v):
    return pltpu.roll(v, 1, 0)


def down_z(v):
    return pltpu.roll(v, 1, 1)


def edges(shape, value):
    p = lax.broadcasted_iota(jnp.int32, shape, 0)
    z = lax.broadcasted_iota(jnp.int32, shape, 1)
    y = lax.bitwise_and(p, BY - 1)
    conditions = (
        p < shape[0] - BY,
        p >= BY,
        y < BY - 1,
        y > 0,
        z < shape[1] - 1,
        z > 0,
    )
    return [jnp.where(c, value, 0.0).astype(jnp.float32) for c in conditions]


def warp_tile(brick, frac_x, frac_y, frac_z, masks, live):
    frac_x, frac_y, frac_z = (f.astype(jnp.float32) for f in (frac_x, frac_y, frac_z))
    high_x, high_y, high_z = frac_x * masks[0], frac_y * masks[2], frac_z * masks[4]
    low_x, low_y, low_z = 1.0 - frac_x, 1.0 - frac_y, 1.0 - frac_z
    low_x, high_x = low_x * live, high_x * live

    def along_z(v):
        return low_z * v + high_z * up_z(v)

    def along_y(v):
        return low_y * along_z(v) + high_y * along_z(up_y(v))

    return low_x * along_y(brick) + high_x * along_y(up_x(brick))


def warp_kernel(spaces, me_ref, counts_ref, slots_ref, *refs):
    parts = refs[:spaces]
    weights_ref, warped_ref, low_ref, high_ref, table, sems = refs[spaces:]
    _, subj_dev, block, plane, depth = weights_ref.shape
    cap = table.shape[0] // spaces
    step, steps = pl.program_id(0), pl.num_programs(0)
    me = me_ref[0]

    @pl.when(step == 0)
    def _():
        copies = [
            pltpu.make_async_copy(part, table.at[pl.ds(k * cap, cap)], sems.at[k])
            for k, part in enumerate(parts)
        ]
        for copy in copies:
            copy.start()
        for copy in copies:
            copy.wait()

    masks = edges((plane, depth), 1.0)

    def tile(r, carry):
        t = step * block + r
        for s in range(subj_dev):
            count = counts_ref[s, 0]
            first = lax.shift_right_logical(count, 1)
            rows = steps * block
            alive = (t < first) | (t >= rows - (count - first))
            live = jnp.where(alive, 1.0, 0.0).astype(jnp.float32)
            slot = lax.bitwise_xor(slots_ref[s, t], me * cap)
            brick = table[slot].astype(jnp.float32)
            warped_ref[s, r] = warp_tile(
                brick, weights_ref[0, s, r], weights_ref[1, s, r], weights_ref[2, s, r], masks, live
            )
        return carry

    lax.fori_loop(0, block, tile, 0, unroll=4)

    @pl.when(step == 0)
    def _():
        low_ref[...] = warped_ref[:, :2]

    @pl.when(step == steps - 1)
    def _():
        high_ref[...] = warped_ref[:, block - 2 :]


def warp(me, counts, slots, parts, weights):
    _, subj_dev, rows, plane, depth = weights.shape
    spaces = len(parts)
    cap = parts[0].shape[0]
    edge = jax.ShapeDtypeStruct((subj_dev, 2, plane, depth), jnp.float32)
    edge_spec = pl.BlockSpec((subj_dev, 2, plane, depth), lambda i: (0, 0, 0, 0))
    return pl.pallas_call(
        functools.partial(warp_kernel, spaces),
        grid=(rows // BLOCK,),
        out_shape=(jax.ShapeDtypeStruct((subj_dev, rows, plane, depth), jnp.float32), edge, edge),
        in_specs=[SMEM] * 3
        + [ANY] * spaces
        + [pl.BlockSpec((3, subj_dev, BLOCK, plane, depth), lambda i: (0, 0, i, 0, 0))],
        out_specs=(
            pl.BlockSpec((subj_dev, BLOCK, plane, depth), lambda i: (0, i, 0, 0)),
            edge_spec,
            edge_spec,
        ),
        scratch_shapes=[
            pltpu.VMEM((spaces * cap, plane, depth), jnp.bfloat16),
            pltpu.SemaphoreType.DMA((spaces,)),
        ],
        compiler_params=params(),
        name="warp",
    )(me, counts, slots, *parts, weights)


def slopes(w, halves):
    return (
        up_x(w) * halves[0] - down_x(w) * halves[1],
        up_y(w) * halves[2] - down_y(w) * halves[3],
        up_z(w) * halves[4] - down_z(w) * halves[5],
    )


def predict(w, g, f):
    return w + (g[0] * f[0] + g[1] * f[1]) + g[2] * f[2]


def update_of(w, f, current, halves):
    g = slopes(w, halves)
    ratio = (predict(w, g, f) - current) / (g[0] * g[0] + g[1] * g[1] + g[2] * g[2] + RIDGE)
    return [g[c] * ratio for c in range(3)]


def smooth(before, here, after, halves):
    rowwise = 0.25 * before + 0.5 * here + 0.25 * after
    return (
        (0.5 * halves[5]) * down_z(rowwise)
        + 0.5 * rowwise
        + (0.5 * halves[4]) * up_z(rowwise)
    )


def update_kernel(warped_ref, field_ref, current_ref, update_ref):
    subj_dev, block, plane, depth = warped_ref.shape
    halves = edges((plane, depth), 0.5)

    def tile(r, carry):
        current = current_ref[r]
        for s in range(subj_dev):
            f = [field_ref[c, s, r] for c in range(3)]
            u = update_of(warped_ref[s, r], f, current, halves)
            for c in range(3):
                update_ref[c, s, r] = u[c]
        return carry

    lax.fori_loop(0, block, tile, 0, unroll=4)


def update(warped, field, current):
    _, subj_dev, rows, plane, depth = field.shape
    five = pl.BlockSpec((3, subj_dev, BLOCK, plane, depth), lambda i: (0, 0, i, 0, 0))
    return pl.pallas_call(
        update_kernel,
        grid=(rows // BLOCK,),
        out_shape=jax.ShapeDtypeStruct(field.shape, jnp.float32),
        in_specs=[
            pl.BlockSpec((subj_dev, BLOCK, plane, depth), lambda i: (0, i, 0, 0)),
            five,
            pl.BlockSpec((BLOCK, plane, depth), lambda i: (i, 0, 0)),
        ],
        out_specs=five,
        compiler_params=params(),
        name="update",
    )(warped, field, current)


def store_sum(keep_ref, send_ref, row, total, core):
    half = total.shape[0] // 2
    low, high = total[:half], total[half:]
    keep_ref[row] = jnp.where(core == 0, low, high)
    send_ref[row] = jnp.where(core == 0, high, low)


def move_kernel(
    core_ref,
    update_ref,
    before_ref,
    after_ref,
    warped_ref,
    field_ref,
    halo_warped_ref,
    halo_field_ref,
    halo_current_ref,
    moved_ref,
    halo_moved_ref,
    keep_ref,
    send_ref,
    halo_update,
):
    subj_dev, block, plane, depth = warped_ref.shape
    step, steps = pl.program_id(0), pl.num_programs(0)
    core = core_ref[0]
    halves = edges((plane, depth), 0.5)

    @pl.when(step == 0)
    def _():
        for s in range(subj_dev):
            for h in range(4):
                f = [halo_field_ref[c, s, h] for c in range(3)]
                u = update_of(halo_warped_ref[s, h], f, halo_current_ref[h], halves)
                for c in range(3):
                    halo_update[c, s, h] = u[c]

    def halo_row(h, out, row, neighbours):
        total = None
        for s in range(subj_dev):
            w = halo_warped_ref[s, h]
            g = slopes(w, halves)
            f = []
            for c in range(3):
                before, here, after = neighbours(c, s)
                f.append(halo_field_ref[c, s, h] - smooth(before, here, after, halves))
                halo_moved_ref[c, s, out] = f[c]
            p = predict(w, g, f)
            total = p if total is None else total + p
        store_sum(keep_ref, send_ref, row, total, core)

    @pl.when(step == 0)
    def _():
        halo_row(
            1,
            0,
            0,
            lambda c, s: (halo_update[c, s, 0], halo_update[c, s, 1], update_ref[c, s, 0]),
        )

    @pl.when(step == steps - 1)
    def _():
        halo_row(
            2,
            1,
            steps * block + 1,
            lambda c, s: (update_ref[c, s, block - 1], halo_update[c, s, 2], halo_update[c, s, 3]),
        )

    def row_of(r, before_of, after_of):
        total = None
        for s in range(subj_dev):
            w = warped_ref[s, r]
            g = slopes(w, halves)
            f = []
            for c in range(3):
                delta = smooth(before_of(c, s), update_ref[c, s, r], after_of(c, s), halves)
                f.append(field_ref[c, s, r] - delta)
                moved_ref[c, s, r] = f[c]
            p = predict(w, g, f)
            total = p if total is None else total + p
        store_sum(keep_ref, send_ref, step * block + r + 1, total, core)

    row_of(
        0,
        lambda c, s: jnp.where(step == 0, halo_update[c, s, 1], before_ref[c, s, 0]),
        lambda c, s: update_ref[c, s, 1],
    )

    def tile(r, carry):
        row_of(
            r, lambda c, s: update_ref[c, s, r - 1], lambda c, s: update_ref[c, s, r + 1]
        )
        return carry

    lax.fori_loop(1, block - 1, tile, 0, unroll=2)
    row_of(
        block - 1,
        lambda c, s: update_ref[c, s, block - 2],
        lambda c, s: jnp.where(step == steps - 1, halo_update[c, s, 2], after_ref[c, s, 0]),
    )


def move(core, updates, warped, field, halo_warped, halo_field, halo_current):
    _, subj_dev, rows, plane, depth = field.shape
    five = pl.BlockSpec((3, subj_dev, BLOCK, plane, depth), lambda i: (0, 0, i, 0, 0))
    line = (3, subj_dev, 1, plane, depth)
    halo_moved = jax.ShapeDtypeStruct((3, subj_dev, 2, plane, depth), jnp.float32)
    sums = jax.ShapeDtypeStruct((rows + 2, plane // 2, depth), jnp.float32)
    return pl.pallas_call(
        move_kernel,
        grid=(rows // BLOCK,),
        out_shape=(
            jax.ShapeDtypeStruct(field.shape, jnp.float32),
            halo_moved,
            sums,
            sums,
        ),
        in_specs=[
            SMEM,
            five,
            pl.BlockSpec(line, lambda i: (0, 0, jnp.maximum(i * BLOCK - 1, 0), 0, 0)),
            pl.BlockSpec(line, lambda i: (0, 0, jnp.minimum(i * BLOCK + BLOCK, rows - 1), 0, 0)),
            pl.BlockSpec((subj_dev, BLOCK, plane, depth), lambda i: (0, i, 0, 0)),
            five,
            VMEM,
            VMEM,
            VMEM,
        ],
        out_specs=(
            five,
            pl.BlockSpec(halo_moved.shape, lambda i: (0, 0, 0, 0, 0)),
            pl.BlockSpec(sums.shape, lambda i: (0, 0, 0)),
            pl.BlockSpec(sums.shape, lambda i: (0, 0, 0)),
        ),
        scratch_shapes=[pltpu.VMEM((3, subj_dev, 4, plane, depth), jnp.float32)],
        compiler_params=params(),
        name="move",
    )(core, updates, updates, updates, warped, field, halo_warped, halo_field, halo_current)


def last_kernel(
    core_ref,
    warped_ref,
    field_ref,
    mine_ref,
    other_ref,
    old_warped_ref,
    old_field_ref,
    halo_warped_ref,
    halo_field_ref,
    moved_ref,
    keep_ref,
    send_ref,
    ring,
):
    subj_dev, block, plane, depth = warped_ref.shape
    step, steps = pl.program_id(0), pl.num_programs(0)
    blocks = steps - 1
    core = core_ref[0]
    halves = edges((plane, depth), 0.5)

    def current_at(row):
        mine, other = mine_ref[row].astype(jnp.float32), other_ref[row].astype(jnp.float32)
        low = jnp.where(core == 0, mine, other)
        high = jnp.where(core == 0, other, mine)
        return jnp.concatenate([low, high], axis=0)

    def halo_update(h, row, place):
        current = current_at(row)
        for s in range(subj_dev):
            f = [halo_field_ref[c, s, h] for c in range(3)]
            u = update_of(halo_warped_ref[s, h + 1], f, current, halves)
            for c in range(3):
                ring[c, s, place] = u[c]

    @pl.when(step == 0)
    def _():
        halo_update(0, 0, block)

    @pl.when(step < blocks)
    def _():
        def tile(r, carry):
            current = current_at(step * block + r + 1)
            for s in range(subj_dev):
                f = [field_ref[c, s, r] for c in range(3)]
                u = update_of(warped_ref[s, r], f, current, halves)
                for c in range(3):
                    ring[c, s, block + 1 + r] = u[c]
            return carry

        lax.fori_loop(0, block, tile, 0, unroll=4)

    @pl.when(step == blocks)
    def _():
        halo_update(1, blocks * block + 1, block + 1)

    @pl.when(step > 0)
    def _():
        def tile(r, carry):
            total = None
            for s in range(subj_dev):
                w = old_warped_ref[s, r]
                g = slopes(w, halves)
                f = []
                for c in range(3):
                    delta = smooth(ring[c, s, r], ring[c, s, r + 1], ring[c, s, r + 2], halves)
                    f.append(old_field_ref[c, s, r] - delta)
                    moved_ref[c, s, r] = f[c]
                p = predict(w, g, f)
                total = p if total is None else total + p
            quarter = plane // 4
            low, high = total[: 2 * quarter], total[2 * quarter :]
            upper = lax.broadcasted_iota(jnp.int32, low.shape, 0) >= quarter
            even = jnp.where(upper, pltpu.roll(high, quarter, 0), low)
            odd = jnp.where(upper, high, pltpu.roll(low, quarter, 0))
            row = (step - 1) * block + r
            keep_ref[row] = jnp.where(core == 0, even, odd)
            send_ref[row] = jnp.where(core == 0, odd, even)
            return carry

        lax.fori_loop(0, block, tile, 0, unroll=2)

    for c in range(3):
        for s in range(subj_dev):
            for r in range(block + 1):
                ring[c, s, r] = ring[c, s, block + r]


def last(core, warped, field, mine, other, halo_warped, halo_field):
    _, subj_dev, rows, plane, depth = field.shape
    blocks = rows // BLOCK
    now = lambda i: jnp.minimum(i, blocks - 1)
    old = lambda i: jnp.maximum(i - 1, 0)
    five = (3, subj_dev, BLOCK, plane, depth)
    four = (subj_dev, BLOCK, plane, depth)
    sums = jax.ShapeDtypeStruct((rows, plane // 2, depth), jnp.float32)
    return pl.pallas_call(
        last_kernel,
        grid=(blocks + 1,),
        out_shape=(jax.ShapeDtypeStruct(field.shape, jnp.float32), sums, sums),
        in_specs=[
            SMEM,
            pl.BlockSpec(four, lambda i: (0, now(i), 0, 0)),
            pl.BlockSpec(five, lambda i: (0, 0, now(i), 0, 0)),
            VMEM,
            VMEM,
            pl.BlockSpec(four, lambda i: (0, old(i), 0, 0)),
            pl.BlockSpec(five, lambda i: (0, 0, old(i), 0, 0)),
            VMEM,
            VMEM,
        ],
        out_specs=(
            pl.BlockSpec(five, lambda i: (0, 0, old(i), 0, 0)),
            pl.BlockSpec(sums.shape, lambda i: (0, 0, 0)),
            pl.BlockSpec(sums.shape, lambda i: (0, 0, 0)),
        ),
        scratch_shapes=[pltpu.VMEM((3, subj_dev, 2 * BLOCK + 1, plane, depth), jnp.float32)],
        compiler_params=params(),
        name="last",
    )(core, warped, field, mine, other, warped, field, halo_warped, halo_field)


def swap(value, axis, mask):
    count = lax.axis_size(axis)
    return lax.ppermute(value, axis, [(i, i ^ mask) for i in range(count)])


def halo(low_rows, high_rows, dim):
    count = lax.axis_size("space")
    forward = [(i, i + 1) for i in range(count - 1)]
    backward = [(i + 1, i) for i in range(count - 1)]
    before = lax.ppermute(high_rows, "space", forward)
    after = lax.ppermute(low_rows, "space", backward)
    return jnp.concatenate([before, after], axis=dim)


def body(images, velocity, weights, template, owners, local_rows, tile_counts):
    spaces = lax.axis_size("space")
    groups = lax.axis_size("subj")
    subj_dev, rows, plane, depth = images.shape
    cap = subj_dev * (2 * rows // spaces)
    subjects = subj_dev * groups
    position = lax.axis_index("subj")
    core = lax.rem(position, 2)[None]
    me = lax.axis_index("space")[None]

    request, slots = plan(tile_counts, owners, local_rows, cap, spaces)
    wanted = lax.all_to_all(request, "space", split_axis=0, concat_axis=0, tiled=True)

    halo_field = halo(velocity[:, :, :2], velocity[:, :, rows - 2 :], 2)
    halo_template = halo(template[:2], template[rows - 2 :], 0)
    ends = jnp.concatenate([template, halo_template], axis=0)
    shares = jnp.stack([ends] + [swap(ends, "subj", k) for k in range(1, groups)])
    order = lax.bitwise_xor(jnp.arange(groups, dtype=jnp.int32), position)
    whole = jnp.moveaxis(shares[order], 0, 1).reshape(rows + 4, plane, depth)

    sends = pick(me, wanted, images.reshape(subj_dev * rows, plane, depth), cap)
    parts = [sends[0]] + [swap(sends[k], "space", k) for k in range(1, spaces)]
    warped, low, high = warp(me, tile_counts, slots, parts, weights)
    halo_warped = halo(low, high, 1)

    updates = update(warped, velocity, whole)
    field, halo_moved, keep, send = move(
        core, updates, warped, velocity, halo_warped, halo_field, whole[rows:]
    )
    share = keep + swap(send, "subj", 1)
    mask = 2
    while mask < groups:
        share = share + swap(share.astype(jnp.bfloat16), "subj", mask).astype(jnp.float32)
        mask = 2 * mask
    mine = (share / subjects).astype(jnp.bfloat16)
    other = swap(mine, "subj", 1)

    field, keep, send = last(core, warped, field, mine, other, halo_warped, halo_moved)
    if groups == 4:
        share = keep + swap(send, "subj", 1)
        chip = lax.div(position, 2)
        quarter = plane // groups
        own = lax.dynamic_slice_in_dim(share, chip * quarter, quarter, 1)
        away = lax.dynamic_slice_in_dim(share, (1 - chip) * quarter, quarter, 1)
        result = (own + swap(away, "subj", 2)) / subjects
    else:
        quarter = plane // 4
        even = jnp.where(core[0] == 0, keep, send)
        odd = jnp.where(core[0] == 0, send, keep)
        total = jnp.concatenate(
            [even[:, :quarter], odd[:, :quarter], even[:, quarter:], odd[:, quarter:]], axis=1
        )
        result = lax.psum_scatter(total, "subj", scatter_dimension=1, tiled=True) / subjects
    return field, result


def solution(mesh):
    in_specs = (
        P("subj", "space", None, None),
        P(None, "subj", "space", None, None),
        P(None, "subj", "space", None, None),
        P("space", "subj", None),
        P("subj", "space", None),
        P("subj", "space"),
        P("subj", "space"),
    )
    out_specs = (P(None, "subj", "space", None, None), P("space", "subj", None))
    return jax.shard_map(body, mesh=mesh, in_specs=in_specs, out_specs=out_specs, check_vma=False)
```

```python
import functools

import jax
import jax.numpy as jnp
from jax import lax
from jax.experimental import pallas as pl
from jax.experimental.pallas import tpu as pltpu
from jax.sharding import PartitionSpec as P

BY = 4
ITERS = 2
RIDGE = 0.25
LANES = 128
LIMIT = 32 * 1024 * 1024
EDGE = 2
CODES = 48
COUNTS = 64

VMEM = pl.BlockSpec(memory_space=pltpu.VMEM)
SMEM = pl.BlockSpec(memory_space=pltpu.SMEM)
ANY = pl.BlockSpec(memory_space=pl.ANY)


def params():
    return pltpu.CompilerParams(vmem_limit_bytes=LIMIT)


def shaped(shape, dtype=jnp.float32):
    return jax.ShapeDtypeStruct(shape, dtype)


def plan_kernel(
    cap, counts_ref, owners_ref, rows_ref, images_ref, request_ref, slots_ref, held_ref, sem
):
    subj_dev, rows = rows_ref.shape
    spaces = request_ref.shape[0]
    fetch = pltpu.make_async_copy(images_ref, held_ref, sem)
    fetch.start()
    t = lax.broadcasted_iota(jnp.int32, (rows, rows), 0)
    u = lax.broadcasted_iota(jnp.int32, (rows, rows), 1)
    eye = t == u
    lane = lax.broadcasted_iota(jnp.int32, (rows, LANES), 1)
    line = lax.broadcasted_iota(jnp.int32, (1, LANES), 1)
    sub = lax.broadcasted_iota(jnp.int32, (spaces, LANES), 0)
    zero = jnp.zeros((rows, rows), jnp.int32)
    request = jnp.zeros((spaces, LANES), jnp.int32)
    extra = jnp.zeros((1, LANES), jnp.int32)
    earlier_subjects = []
    for s in range(subj_dev):
        count = counts_ref[0, s]
        first = lax.shift_right_logical(count, 1)
        owner_u = jnp.broadcast_to(owners_ref[s], (rows, rows))
        row_u = jnp.broadcast_to(rows_ref[s : s + 1, :], (rows, rows))
        owner_t = jnp.broadcast_to(
            jnp.sum(jnp.where(eye, owner_u, zero), axis=1, keepdims=True), (rows, rows)
        )
        row_t = jnp.broadcast_to(
            jnp.sum(jnp.where(eye, row_u, zero), axis=1, keepdims=True), (rows, rows)
        )
        last = rows - (count - first)
        alive_t = (t < first) | (t >= last)
        alive_u = (u < first) | (u >= last)
        same_owner = owner_t == owner_u
        same = same_owner & (row_t == row_u)
        dup_u = jnp.sum(jnp.where(same & alive_t & (t < u), 1, 0), axis=0, keepdims=True)
        dup_t = jnp.sum(jnp.where(same & alive_u & (u < t), 1, 0), axis=1, keepdims=True)
        first_u = alive_u & jnp.broadcast_to(dup_u == 0, (rows, rows))
        first_t = alive_t & jnp.broadcast_to(dup_t == 0, (rows, rows))
        place = jnp.sum(jnp.where(same_owner & first_u & (u < t), 1, 0), axis=1, keepdims=True)
        for owner_v, first_v in earlier_subjects:
            place = place + jnp.sum(
                jnp.where((owner_t == owner_v) & first_v, 1, 0), axis=1, keepdims=True
            )
        earlier_subjects.append((owner_u, first_u))
        slot_t = owner_t * cap + place
        slots_ref[s : s + 1, :] = jnp.sum(
            jnp.where(same & first_t & alive_u, slot_t, zero), axis=0, keepdims=True
        )
        wide_first = jnp.broadcast_to(first_t[:, :1], (rows, LANES))
        wide_owner = jnp.broadcast_to(owner_t[:, :1], (rows, LANES))
        wide_place = jnp.broadcast_to(place, (rows, LANES))
        wide_row = jnp.broadcast_to(row_t[:, :1], (rows, LANES)) + s * rows
        wide_tile = lax.broadcasted_iota(jnp.int32, (rows, LANES), 0)
        hit = jnp.where(wide_first & (wide_place == lane), wide_row, 0)
        for o in range(spaces):
            asked = jnp.sum(jnp.where(wide_owner == o, hit, 0), axis=0, keepdims=True)
            request = request + jnp.where(sub == o, asked, 0)
        counted = jnp.where(wide_first & (wide_owner == lane - COUNTS), 1, 0)
        extra = extra + jnp.sum(counted, axis=0, keepdims=True)
        for side, begin in enumerate((0, rows - EDGE)):
            place = CODES + (side * subj_dev + s) * EDGE
            code = jnp.where(
                wide_tile - begin == lane - place, wide_owner * (subj_dev * rows) + wide_row, 0
            )
            code = jnp.sum(code, axis=0, keepdims=True)
            extra = extra + jnp.where((line >= place) & (line < place + EDGE), code, 0)
    request_ref[...] = request + jnp.broadcast_to(extra, request.shape)
    fetch.wait()


def plan(counts, owners, local_rows, images, cap, spaces):
    subj_dev, rows = local_rows.shape
    return pl.pallas_call(
        functools.partial(plan_kernel, cap),
        out_shape=(
            shaped((spaces, LANES), jnp.int32),
            shaped((subj_dev, rows), jnp.int32),
            shaped(images.shape, images.dtype),
        ),
        in_specs=[SMEM, VMEM, VMEM, ANY],
        out_specs=(VMEM, VMEM, VMEM),
        scratch_shapes=[pltpu.SemaphoreType.DMA],
        compiler_params=params(),
        name="plan",
    )(counts, owners, local_rows, images)


def edge_codes(wanted_ref, me, subj_dev):
    spaces = wanted_ref.shape[0]
    before, after = jnp.maximum(me - 1, 0), jnp.minimum(me + 1, spaces - 1)
    found = []
    for i in range(subj_dev * EDGE):
        found.append((wanted_ref[before, CODES + subj_dev * EDGE + i], me > 0))
    for i in range(subj_dev * EDGE):
        found.append((wanted_ref[after, CODES + i], me < spaces - 1))
    return found


def pick_kernel(cap, base, per_owner, subj_dev, me_ref, wanted_ref, images_ref, *refs):
    spaces = wanted_ref.shape[0]
    mains, overs, (edge_slots, held, used) = refs[:spaces], refs[spaces:-3], refs[-3:]
    total = held.shape[0] - 1
    me = me_ref[0]
    for k in range(spaces):
        target = lax.bitwise_xor(me, k)
        for c in range(cap):
            held[c] = images_ref[wanted_ref[target, c]]
        place = wanted_ref[target, COUNTS + me]
        for code, valid in edge_codes(wanted_ref, target, subj_dev):
            owner = lax.div(code, per_owner)
            held[place] = images_ref[code - owner * per_owner]
            place = place + jnp.where(valid & (owner == me), 1, 0)
        size = mains[k].shape[0]
        for c in range(size):
            mains[k][c] = held[c]
        if k >= base:
            for c in range(total - size):
                overs[k - base][c] = held[size + c]
    for o in range(spaces):
        used[o] = wanted_ref[me, COUNTS + o]
    for i, (code, valid) in enumerate(edge_codes(wanted_ref, me, subj_dev)):
        owner = lax.div(code, per_owner)
        owner = jnp.where(valid, owner, 0)
        place = used[owner]
        edge_slots[i] = jnp.where(valid, lax.bitwise_xor(owner, me) * total + place, 0)
        used[owner] = place + jnp.where(valid, 1, 0)


def pick(me, wanted, images, cap, sizes, per_owner, subj_dev):
    spaces = wanted.shape[0]
    total = cap + 2 * EDGE * subj_dev
    base = sizes.index(min(sizes))
    tile = images.shape[1:]
    outs = [shaped((n,) + tile, images.dtype) for n in sizes]
    outs += [shaped((total - n,) + tile, images.dtype) for n in sizes[base:]]
    got = pl.pallas_call(
        functools.partial(pick_kernel, cap, base, per_owner, subj_dev),
        out_shape=outs + [shaped((2 * EDGE * subj_dev,), jnp.int32)],
        in_specs=[SMEM, SMEM, VMEM],
        out_specs=[VMEM] * len(outs) + [SMEM],
        scratch_shapes=[
            pltpu.VMEM((total + 1,) + tile, images.dtype),
            pltpu.SMEM((spaces,), jnp.int32),
        ],
        compiler_params=params(),
        name="pick",
    )(me, wanted, images)
    return got[:spaces], got[spaces:-1], got[-1]


def check_kernel(base, size, per_owner, subj_dev, wanted_ref, over_ref):
    spaces = wanted_ref.shape[0]

    def target(d, worst):
        codes = [
            (jnp.where(valid, lax.div(code, per_owner), -1))
            for code, valid in edge_codes(wanted_ref, d, subj_dev)
        ]

        def owner(k, worst):
            o = lax.bitwise_xor(d, k)
            need = wanted_ref[d, COUNTS + o]
            for code in codes:
                need = need + jnp.where(code == o, 1, 0)
            return jnp.maximum(worst, need)

        return lax.fori_loop(base, spaces, owner, worst)

    worst = lax.fori_loop(0, spaces, target, jnp.int32(0))
    over_ref[...] = jnp.broadcast_to(jnp.where(worst > size, 1, 0), over_ref.shape)


def check(wanted, base, size, per_owner, subj_dev):
    return pl.pallas_call(
        functools.partial(check_kernel, base, size, per_owner, subj_dev),
        out_shape=shaped((8, LANES), jnp.int32),
        in_specs=[SMEM],
        out_specs=VMEM,
        compiler_params=params(),
        name="check",
    )(wanted)


def stage_kernel(*refs):
    (velocity_ref, weights_ref, whole_ref) = refs[:3]
    (v_ref, w_ref, low_ref, high_ref, sems) = refs[3:]
    copies = [
        pltpu.make_async_copy(velocity_ref, v_ref, sems.at[0]),
        pltpu.make_async_copy(weights_ref, w_ref, sems.at[1]),
    ]
    for copy in copies:
        copy.start()
    for copy in copies:
        copy.wait()
    _, subj_dev, rows = v_ref.shape[:3]
    for out, begin in ((low_ref, 0), (high_ref, rows - EDGE)):
        i = 0
        for c in range(3):
            for s in range(subj_dev):
                for r in range(EDGE):
                    out[i] = v_ref[c, s, begin + r].astype(out.dtype)
                    out[i + 1] = w_ref[c, s, begin + r]
                    i = i + 2
        for r in range(EDGE):
            value = whole_ref[begin + r]
            rounded = value.astype(out.dtype)
            out[i] = rounded
            out[i + 1] = (value - rounded.astype(jnp.float32)).astype(out.dtype)
            i = i + 2


def stage(velocity, weights, whole):
    subj_dev = velocity.shape[1]
    edge = shaped((2 * EDGE * (3 * subj_dev + 1),) + velocity.shape[3:], weights.dtype)
    return pl.pallas_call(
        stage_kernel,
        out_shape=(
            shaped(velocity.shape, velocity.dtype),
            shaped(weights.shape, weights.dtype),
            edge,
            edge,
        ),
        in_specs=[ANY, ANY, VMEM],
        out_specs=(VMEM,) * 4,
        scratch_shapes=[pltpu.SemaphoreType.DMA((2,))],
        compiler_params=params(),
        name="stage",
    )(velocity, weights, whole)


def up_x(v):
    return pltpu.roll(v, v.shape[0] - BY, 0)


def up_y(v):
    return pltpu.roll(v, v.shape[0] - 1, 0)


def up_z(v):
    return pltpu.roll(v, v.shape[1] - 1, 1)


def down_x(v):
    return pltpu.roll(v, BY, 0)


def down_y(v):
    return pltpu.roll(v, 1, 0)


def down_z(v):
    return pltpu.roll(v, 1, 1)


def inside(shape, value):
    p = lax.broadcasted_iota(jnp.int32, shape, 0)
    z = lax.broadcasted_iota(jnp.int32, shape, 1)
    y = lax.bitwise_and(p, BY - 1)
    conditions = (
        p < shape[0] - BY,
        p >= BY,
        y < BY - 1,
        y > 0,
        z < shape[1] - 1,
        z > 0,
    )
    return [jnp.where(c, value, 0.0).astype(jnp.float32) for c in conditions]


def warp_tile(brick, fractions, masks, live):
    frac_x, frac_y, frac_z = (f.astype(jnp.float32) for f in fractions)
    high_x, high_y, high_z = frac_x * masks[0], frac_y * masks[2], frac_z * masks[4]
    low_x, low_y, low_z = 1.0 - frac_x, 1.0 - frac_y, 1.0 - frac_z
    low_x, high_x = low_x * live, high_x * live

    def along_z(v):
        return low_z * v + high_z * up_z(v)

    def along_y(v):
        return low_y * along_z(v) + high_y * along_z(up_y(v))

    return low_x * along_y(brick) + high_x * along_y(up_x(brick))


def slopes(w, halves):
    return (
        up_x(w) * halves[0] - down_x(w) * halves[1],
        up_y(w) * halves[2] - down_y(w) * halves[3],
        up_z(w) * halves[4] - down_z(w) * halves[5],
    )


def predict(w, g, f):
    return w + (g[0] * f[0] + g[1] * f[1]) + g[2] * f[2]


def smooth(before, here, after, masks):
    rowwise = (before + after) + (here + here)
    return (down_z(rowwise) * masks[5] + up_z(rowwise) * masks[4]) + (rowwise + rowwise)


def first_kernel(spaces, base, *refs):
    me_ref, core_ref, counts_ref, slots_ref, edge_slots_ref = refs[:5]
    mains = refs[5 : 5 + spaces]
    overs = refs[5 + spaces : 5 + 2 * spaces - base]
    weights_ref, velocity_ref, whole_ref, before_ref, after_ref = refs[5 + 2 * spaces - base :][:5]
    warped_ref, slopes_ref, scale_ref, field_ref, keep_ref, send_ref, table, update = refs[-8:]
    _, subj_dev, rows, plane, depth = weights_ref.shape
    total = table.shape[0] // spaces
    cap = total - 2 * EDGE * subj_dev
    me, core = me_ref[0], core_ref[0]
    masks, halves = inside((plane, depth), 1.0), inside((plane, depth), 0.5)

    for k in range(spaces):
        size = mains[k].shape[0]
        for c in range(size):
            table[k * total + c] = mains[k][c]
        if k >= base:
            for c in range(total - size):
                table[k * total + size + c] = overs[k - base][c]

    def tile(s, e, brick, fractions, live, f, current):
        w = warp_tile(brick.astype(jnp.float32), fractions, masks, live)
        g = slopes(w, halves)
        scale = 0.0625 / (g[0] * g[0] + g[1] * g[1] + g[2] * g[2] + RIDGE)
        ratio = (predict(w, g, f) - current) * scale
        warped_ref[s, e] = w
        scale_ref[s, e] = scale
        for c in range(3):
            slopes_ref[c, s, e] = g[c]
            update[c, s, e] = g[c] * ratio

    def row(r, carry):
        current = whole_ref[r]
        for s in range(subj_dev):
            count = counts_ref[0, s]
            first = lax.shift_right_logical(count, 1)
            alive = (r < first) | (r >= rows - (count - first))
            live = jnp.where(alive, 1.0, 0.0).astype(jnp.float32)
            wanted = slots_ref[s, r]
            owner = lax.div(wanted, cap)
            slot = lax.bitwise_xor(owner, me) * total + (wanted - owner * cap)
            tile(
                s,
                r + EDGE,
                table[slot],
                [weights_ref[c, s, r] for c in range(3)],
                live,
                [velocity_ref[c, s, r] for c in range(3)],
                current,
            )
        return carry

    lax.fori_loop(0, rows, row, 0, unroll=2)

    for side, (ref, there, e0) in enumerate(
        ((before_ref, me > 0, 0), (after_ref, me < spaces - 1, rows + EDGE))
    ):
        live = jnp.where(there, 1.0, 0.0).astype(jnp.float32)
        for r in range(EDGE):
            at = 2 * EDGE * 3 * subj_dev + 2 * r
            current = ref[at].astype(jnp.float32) + ref[at + 1].astype(jnp.float32)
            for s in range(subj_dev):
                at = [2 * ((c * subj_dev + s) * EDGE + r) for c in range(3)]
                tile(
                    s,
                    e0 + r,
                    table[edge_slots_ref[(side * subj_dev + s) * EDGE + r]],
                    [ref[a + 1] for a in at],
                    live,
                    [ref[a].astype(jnp.float32) for a in at],
                    current,
                )

    def moved(e, old):
        total_p = None
        for s in range(subj_dev):
            g = [slopes_ref[c, s, e] for c in range(3)]
            f = []
            for c in range(3):
                delta = smooth(update[c, s, e - 1], update[c, s, e], update[c, s, e + 1], masks)
                f.append(old(c, s) - delta)
                field_ref[c, s, e - 1] = f[c]
            p = predict(warped_ref[s, e], g, f)
            total_p = p if total_p is None else total_p + p
        half = plane // 2
        low, high = total_p[:half], total_p[half:]
        keep_ref[e - 1] = jnp.where(core == 0, low, high)
        send_ref[e - 1] = jnp.where(core == 0, high, low)

    def edge_field(ref, r):
        return lambda c, s: ref[2 * ((c * subj_dev + s) * EDGE + r)].astype(jnp.float32)

    moved(EDGE - 1, edge_field(before_ref, EDGE - 1))
    moved(rows + EDGE, edge_field(after_ref, 0))

    def move(r, carry):
        moved(r + EDGE, lambda c, s: velocity_ref[c, s, r])
        return carry

    lax.fori_loop(0, rows, move, 0, unroll=2)


def first(me, core, counts, slots, edge_slots, mains, overs, weights, velocity, whole, before, after):
    _, subj_dev, rows, plane, depth = velocity.shape
    spaces = len(mains)
    base = spaces - len(overs)
    total = mains[0].shape[0]
    long = rows + 2 * EDGE
    sums = shaped((rows + 2, plane // 2, depth))
    arrays = [*mains, *overs, weights, velocity, whole, before, after]
    return pl.pallas_call(
        functools.partial(first_kernel, spaces, base),
        out_shape=(
            shaped((subj_dev, long, plane, depth)),
            shaped((3, subj_dev, long, plane, depth)),
            shaped((subj_dev, long, plane, depth)),
            shaped((3, subj_dev, rows + 2, plane, depth)),
            sums,
            sums,
        ),
        in_specs=[SMEM] * 5 + [VMEM] * len(arrays),
        out_specs=(VMEM,) * 6,
        scratch_shapes=[
            pltpu.VMEM((spaces * total, plane, depth), weights.dtype),
            pltpu.VMEM((3, subj_dev, long, plane, depth), jnp.float32),
        ],
        compiler_params=params(),
        name="first",
    )(me, core, counts, slots, edge_slots, *arrays)


def last_kernel(
    core_ref,
    mine_ref,
    other_ref,
    warped_ref,
    slopes_ref,
    scale_ref,
    field_ref,
    out_ref,
    keep_ref,
    send_ref,
    update,
    out,
    sems,
):
    _, subj_dev, rows, plane, depth = out.shape
    core = core_ref[0]
    masks = inside((plane, depth), 1.0)
    chunks = sems.shape[0]
    chunk = rows // chunks

    def renew(i, carry):
        mine, other = mine_ref[i].astype(jnp.float32), other_ref[i].astype(jnp.float32)
        current = jnp.concatenate(
            [jnp.where(core == 0, mine, other), jnp.where(core == 0, other, mine)], axis=0
        )
        for s in range(subj_dev):
            g = [slopes_ref[c, s, i + 1] for c in range(3)]
            f = [field_ref[c, s, i] for c in range(3)]
            ratio = (predict(warped_ref[s, i + 1], g, f) - current) * scale_ref[s, i + 1]
            for c in range(3):
                update[c, s, i] = g[c] * ratio
        return carry

    lax.fori_loop(0, rows + 2, renew, 0, unroll=3)

    def move(r, carry):
        total = None
        for s in range(subj_dev):
            g = [slopes_ref[c, s, r + EDGE] for c in range(3)]
            f = []
            for c in range(3):
                delta = smooth(update[c, s, r], update[c, s, r + 1], update[c, s, r + 2], masks)
                f.append(field_ref[c, s, r + 1] - delta)
                out[c, s, r] = f[c]
            p = predict(warped_ref[s, r + EDGE], g, f)
            total = p if total is None else total + p
        quarter = plane // 4
        low, high = total[: 2 * quarter], total[2 * quarter :]
        upper = lax.broadcasted_iota(jnp.int32, low.shape, 0) >= quarter
        even = jnp.where(upper, pltpu.roll(high, quarter, 0), low)
        odd = jnp.where(upper, high, pltpu.roll(low, quarter, 0))
        keep_ref[r] = jnp.where(core == 0, even, odd)
        send_ref[r] = jnp.where(core == 0, odd, even)
        return carry

    copies = []
    for i in range(chunks):
        lax.fori_loop(i * chunk, (i + 1) * chunk, move, 0, unroll=2)
        part = pl.ds(i * chunk, chunk)
        copy = pltpu.make_async_copy(out.at[:, :, part], out_ref.at[:, :, part], sems.at[i])
        copy.start()
        copies.append(copy)
    for copy in copies:
        copy.wait()


def last(core, mine, other, warped, slopes_all, scale, field, rows):
    _, subj_dev, _, plane, depth = field.shape
    shape = (3, subj_dev, rows, plane, depth)
    sums = shaped((rows, plane // 2, depth))
    return pl.pallas_call(
        last_kernel,
        out_shape=(shaped(shape), sums, sums),
        in_specs=[SMEM] + [VMEM] * 6,
        out_specs=(ANY, VMEM, VMEM),
        scratch_shapes=[
            pltpu.VMEM(field.shape, jnp.float32),
            pltpu.VMEM(shape, jnp.float32),
            pltpu.SemaphoreType.DMA((4,)),
        ],
        compiler_params=params(),
        name="last",
    )(core, mine, other, warped, slopes_all, scale, field)


def swap(value, axis, mask):
    count = lax.axis_size(axis)
    return lax.ppermute(value, axis, [(i, i ^ mask) for i in range(count)])


def body(images, velocity, weights, template, owners, local_rows, tile_counts):
    spaces = lax.axis_size("space")
    groups = lax.axis_size("subj")
    subj_dev, rows, plane, depth = images.shape
    cap = subj_dev * (2 * rows // spaces)
    total = cap + 2 * EDGE * subj_dev
    subjects = subj_dev * groups
    position = lax.axis_index("subj")
    core = lax.rem(position, 2)[None]
    me = lax.axis_index("space")[None]
    counts = jnp.swapaxes(tile_counts, 0, 1)

    request, slots, held = plan(
        counts,
        jnp.swapaxes(owners, 1, 2),
        local_rows,
        images.reshape(subj_dev * rows, plane, depth),
        cap,
        spaces,
    )
    wanted = lax.all_to_all(request, "space", split_axis=0, concat_axis=0, tiled=True)

    base = spaces // 2
    short = cap - cap // 8
    sizes = [total] * base + [short] * (spaces - base)
    mains, overs, edge_slots = pick(me, wanted, held, cap, sizes, subj_dev * rows, subj_dev)
    far = [swap(mains[k], "space", k) for k in range(base, spaces)]

    flag = check(wanted, base, short, subj_dev * rows, subj_dev)
    mask = 1
    while mask < groups:
        flag = jnp.maximum(flag, swap(flag, "subj", mask))
        mask = 2 * mask

    def second(parts):
        return [swap(part, "space", base + i) for i, part in enumerate(parts)]

    overs = lax.cond(flag[0, 0] > 0, second, lambda parts: list(parts), list(overs))

    shares = jnp.stack([template] + [swap(template, "subj", k) for k in range(1, groups)])
    order = lax.bitwise_xor(jnp.arange(groups, dtype=jnp.int32), position)
    whole = jnp.moveaxis(shares[order], 0, 1).reshape(rows, plane, depth)
    held_velocity, held_weights, low, high = stage(velocity, weights, whole)
    forward = [(i, i + 1) for i in range(spaces - 1)]
    backward = [(i + 1, i) for i in range(spaces - 1)]
    before = lax.ppermute(high, "space", forward)
    after = lax.ppermute(low, "space", backward)
    near = [mains[0]] + [swap(mains[k], "space", k) for k in range(1, base)]

    warped, slopes_all, scale, field, keep, send = first(
        me,
        core,
        counts,
        slots,
        edge_slots,
        near + far,
        overs,
        held_weights,
        held_velocity,
        whole,
        before,
        after,
    )
    share = keep + swap(send, "subj", 1)
    mask = 2
    while mask < groups:
        share = share + swap(share.astype(jnp.bfloat16), "subj", mask).astype(jnp.float32)
        mask = 2 * mask
    mine = (share / subjects).astype(jnp.bfloat16)
    other = swap(mine, "subj", 1)

    field, keep, send = last(core, mine, other, warped, slopes_all, scale, field, rows)
    if groups == 4:
        share = keep + swap(send, "subj", 1)
        chip = lax.div(position, 2)
        quarter = plane // groups
        own = lax.dynamic_slice_in_dim(share, chip * quarter, quarter, 1)
        away = lax.dynamic_slice_in_dim(share, (1 - chip) * quarter, quarter, 1)
        result = (own + swap(away, "subj", 2)) / subjects
    else:
        quarter = plane // 4
        even = jnp.where(core[0] == 0, keep, send)
        odd = jnp.where(core[0] == 0, send, keep)
        full = jnp.concatenate(
            [even[:, :quarter], odd[:, :quarter], even[:, quarter:], odd[:, quarter:]], axis=1
        )
        result = lax.psum_scatter(full, "subj", scatter_dimension=1, tiled=True) / subjects
    return field, result


def solution(mesh):
    in_specs = (
        P("subj", "space", None, None),
        P(None, "subj", "space", None, None),
        P(None, "subj", "space", None, None),
        P("space", "subj", None),
        P("subj", "space", None),
        P("subj", "space"),
        P("subj", "space"),
    )
    out_specs = (P(None, "subj", "space", None, None), P("space", "subj", None))
    return jax.shard_map(body, mesh=mesh, in_specs=in_specs, out_specs=out_specs, check_vma=False)
```

```python
import functools

import jax
import jax.numpy as jnp
from jax import lax
from jax.experimental import pallas as pl
from jax.experimental.pallas import tpu as pltpu
from jax.sharding import PartitionSpec as P

BY = 4
ITERS = 2
RIDGE = 0.25
LANES = 128
LIMIT = 24 * 1024 * 1024
EDGE = 2
CODES = 48
HEAD = 8
COUNTS = 64
SHIFT = 8

VMEM = pl.BlockSpec(memory_space=pltpu.VMEM)
SMEM = pl.BlockSpec(memory_space=pltpu.SMEM)
ANY = pl.BlockSpec(memory_space=pl.ANY)
SMALL = pl.CostEstimate(flops=0, bytes_accessed=0, transcendentals=0)


def params():
    return pltpu.CompilerParams(vmem_limit_bytes=LIMIT)


def shaped(shape, dtype=jnp.float32):
    return jax.ShapeDtypeStruct(shape, dtype)


def in_hbm(value):
    return pltpu.with_memory_space_constraint(value, pltpu.HBM)


def in_vmem(value):
    return pltpu.with_memory_space_constraint(value, pltpu.VMEM)


def plan_kernel(
    cap,
    counts_in,
    owners_in,
    rows_in,
    images_ref,
    template_ref,
    request_ref,
    slots_ref,
    held_ref,
    counts_ref,
    owners_ref,
    rows_ref,
    ends_ref,
    sems,
):
    subj_dev, rows = rows_ref.shape
    spaces = request_ref.shape[0]
    share = template_ref.shape[1]
    me = lax.axis_index("space")
    copies = [
        pltpu.make_async_copy(source, target, sems.at[i])
        for i, (source, target) in enumerate(
            (
                (counts_in, counts_ref),
                (owners_in, owners_ref),
                (rows_in, rows_ref),
                (template_ref.at[pl.ds(0, EDGE)], ends_ref.at[0]),
                (template_ref.at[pl.ds(rows - EDGE, EDGE)], ends_ref.at[1]),
                (images_ref, held_ref),
            )
        )
    ]
    for copy in copies:
        copy.start()
    for copy in copies[:3]:
        copy.wait()
    t = lax.broadcasted_iota(jnp.int32, (rows, rows), 0)
    u = lax.broadcasted_iota(jnp.int32, (rows, rows), 1)
    eye = t == u
    lane = lax.broadcasted_iota(jnp.int32, (rows, LANES), 1)
    line = lax.broadcasted_iota(jnp.int32, (1, LANES), 1)
    sub = lax.broadcasted_iota(jnp.int32, (spaces, LANES), 0)
    zero = jnp.zeros((rows, rows), jnp.int32)
    request = jnp.zeros((spaces, LANES), jnp.int32)
    extra = jnp.zeros((1, LANES), jnp.int32)
    earlier_subjects = []
    for s in range(subj_dev):
        count = counts_ref[0, s]
        first = lax.shift_right_logical(count, 1)
        owner_u = jnp.broadcast_to(owners_ref[s], (rows, rows))
        row_u = jnp.broadcast_to(rows_ref[s : s + 1, :], (rows, rows))
        owner_t = jnp.broadcast_to(
            jnp.sum(jnp.where(eye, owner_u, zero), axis=1, keepdims=True), (rows, rows)
        )
        row_t = jnp.broadcast_to(
            jnp.sum(jnp.where(eye, row_u, zero), axis=1, keepdims=True), (rows, rows)
        )
        last = rows - (count - first)
        alive_t = (t < first) | (t >= last)
        alive_u = (u < first) | (u >= last)
        same_owner = owner_t == owner_u
        same = same_owner & (row_t == row_u)
        dup_u = jnp.sum(jnp.where(same & alive_t & (t < u), 1, 0), axis=0, keepdims=True)
        dup_t = jnp.sum(jnp.where(same & alive_u & (u < t), 1, 0), axis=1, keepdims=True)
        first_u = alive_u & jnp.broadcast_to(dup_u == 0, (rows, rows))
        first_t = alive_t & jnp.broadcast_to(dup_t == 0, (rows, rows))
        place = jnp.sum(jnp.where(same_owner & first_u & (u < t), 1, 0), axis=1, keepdims=True)
        for owner_v, first_v in earlier_subjects:
            place = place + jnp.sum(
                jnp.where((owner_t == owner_v) & first_v, 1, 0), axis=1, keepdims=True
            )
        earlier_subjects.append((owner_u, first_u))
        slot_t = owner_t * cap + place
        slots_ref[s : s + 1, :] = jnp.sum(
            jnp.where(same & first_t & alive_u, slot_t, zero), axis=0, keepdims=True
        )
        wide_first = jnp.broadcast_to(first_t[:, :1], (rows, LANES))
        wide_owner = jnp.broadcast_to(owner_t[:, :1], (rows, LANES))
        wide_place = jnp.broadcast_to(place, (rows, LANES))
        wide_row = jnp.broadcast_to(row_t[:, :1], (rows, LANES)) + s * rows
        wide_tile = lax.broadcasted_iota(jnp.int32, (rows, LANES), 0)
        hit = jnp.where(wide_first & (wide_place == lane), wide_row, 0)
        for o in range(spaces):
            asked = jnp.sum(jnp.where(wide_owner == o, hit, 0), axis=0, keepdims=True)
            request = request + jnp.where(sub == o, asked, 0)
        counted = jnp.where(wide_first & (wide_owner == lane - COUNTS), 1, 0)
        extra = extra + jnp.sum(counted, axis=0, keepdims=True)
        for side, begin in enumerate((0, rows - EDGE)):
            place = CODES + (side * subj_dev + s) * EDGE
            code = jnp.where(
                wide_tile - begin == lane - place, lax.shift_left(wide_owner, SHIFT) + wide_row, 0
            )
            code = jnp.sum(code, axis=0, keepdims=True)
            extra = extra + jnp.where((line >= place) & (line < place + EDGE), code, 0)
    request = (request + jnp.broadcast_to(extra, request.shape)).astype(jnp.float32)
    for copy in copies[3:]:
        copy.wait()
    for o in range(spaces):
        request_ref[o, :HEAD] = jnp.broadcast_to(request[o : o + 1], (HEAD, LANES))
        for r in range(EDGE):
            at = HEAD + r * share
            request_ref[o, at : at + share] = jnp.where(o < me, ends_ref[0, r], ends_ref[1, r])
        if HEAD + EDGE * share < request_ref.shape[1]:
            rest = request_ref.shape[1] - HEAD - EDGE * share
            request_ref[o, HEAD + EDGE * share :] = jnp.zeros((rest, LANES), jnp.float32)


def plan(counts, owners, local_rows, images, template, cap, spaces):
    subj_dev, rows = local_rows.shape
    share = template.shape[1]
    lines = HEAD + -(-EDGE * share // 8) * 8
    return pl.pallas_call(
        functools.partial(plan_kernel, cap),
        out_shape=(
            shaped((spaces, lines, LANES)),
            shaped((subj_dev, rows), jnp.int32),
            pltpu.VMEM(images.shape, images.dtype),
        ),
        in_specs=[ANY] * 5,
        out_specs=(VMEM, VMEM, VMEM),
        scratch_shapes=[
            pltpu.SMEM(counts.shape, jnp.int32),
            pltpu.VMEM(owners.shape, jnp.int32),
            pltpu.VMEM(local_rows.shape, jnp.int32),
            pltpu.VMEM((2, EDGE, share, LANES), jnp.float32),
            pltpu.SemaphoreType.DMA((6,)),
        ],
        compiler_params=params(),
        name="plan",
    )(*map(in_hbm, (counts, owners, local_rows, images, template)))


def edge_codes(wanted_ref, me, subj_dev):
    spaces = wanted_ref.shape[0]
    before, after = jnp.maximum(me - 1, 0), jnp.minimum(me + 1, spaces - 1)
    found = []
    for i in range(subj_dev * EDGE):
        found.append((wanted_ref[before, CODES + subj_dev * EDGE + i], me > 0))
    for i in range(subj_dev * EDGE):
        found.append((wanted_ref[after, CODES + i], me < spaces - 1))
    return found


def crowded(wanted, base, size, subj_dev):
    spaces, lanes = wanted.shape
    d = lax.broadcasted_iota(jnp.int32, (spaces, lanes), 0)
    owner = lax.broadcasted_iota(jnp.int32, (spaces, lanes), 1) - COUNTS
    need = wanted
    for side in range(2):
        codes = pltpu.roll(wanted, 1 if side == 0 else spaces - 1, 0)
        valid = d > 0 if side == 0 else d < spaces - 1
        begin = CODES + (subj_dev * EDGE if side == 0 else 0)
        for i in range(subj_dev * EDGE):
            code = jnp.broadcast_to(codes[:, begin + i : begin + i + 1], (spaces, lanes))
            hit = valid & (lax.shift_right_logical(code, SHIFT) == owner)
            need = need + jnp.where(hit, 1, 0)
    pair = (owner >= 0) & (owner < spaces) & (lax.bitwise_xor(owner, d) >= base)
    over = jnp.where(pair & (need > size), 1.0, 0.0)
    return jnp.max(jnp.max(over, axis=0, keepdims=True), axis=1, keepdims=True)


def pick_kernel(cap, base, total, answers_ref, images_ref, template_ref, velocity_ref, weights_ref, *refs):
    spaces = answers_ref.shape[0]
    sends, overs = refs[:spaces], refs[spaces : 2 * spaces - base]
    edge_slots, side_ref, ends_ref, requests_ref, wanted_ref, used, v_ref, w_ref, sems = refs[-9:]
    rows, share = template_ref.shape[:2]
    subj_dev = velocity_ref.shape[1]
    me = lax.axis_index("space")
    odd = lax.bitwise_and(me, 1)
    fetches = [pltpu.make_async_copy(template_ref, ends_ref.at[pl.ds(0, rows)], sems.at[0])]
    for side, begin in enumerate((0, rows - EDGE)):
        part = pl.ds(begin, EDGE)
        place = lax.bitwise_xor(odd, 1 - side)
        for i, (source, target) in enumerate(((velocity_ref, v_ref), (weights_ref, w_ref))):
            fetches.append(
                pltpu.make_async_copy(
                    source.at[:, :, part], target.at[place], sems.at[2 + 2 * side + i]
                )
            )
    for copy in fetches:
        copy.start()
    for d in range(spaces):
        requests_ref[d : d + 1] = answers_ref[d, :1].astype(jnp.int32)
    move = pltpu.make_async_copy(requests_ref, wanted_ref, sems.at[1])
    move.start()
    for side, neighbour in enumerate((jnp.maximum(me - 1, 0), jnp.minimum(me + 1, spaces - 1))):
        for r in range(EDGE):
            at = HEAD + r * share
            ends_ref[rows + side * EDGE + r] = answers_ref[neighbour, at : at + share]
    move.wait()
    for k in range(spaces):
        target = lax.bitwise_xor(me, k)
        size = sends[k].shape[0] if k >= base else total

        def put(c, brick, k=k, size=size):
            if isinstance(c, int):
                ref, c = (sends[k], c) if c < size else (overs[k - base], c - size)
                ref[c] = brick
            elif k < base:
                sends[k][c] = brick
            else:

                @pl.when(c < size)
                def _():
                    sends[k][c] = brick

                @pl.when(c >= size)
                def _():
                    overs[k - base][c - size] = brick

        for c in range(cap):
            put(c, images_ref[wanted_ref[target, c]])
        place = wanted_ref[target, COUNTS + me]
        for code, valid in edge_codes(wanted_ref, target, subj_dev):
            mine = valid & (lax.shift_right_logical(code, SHIFT) == me)

            @pl.when(mine)
            def _(code=code, place=place, put=put):
                put(place, images_ref[lax.bitwise_and(code, (1 << SHIFT) - 1)])

            place = place + jnp.where(mine, 1, 0)
    ends_ref[rows + 2 * EDGE] = jnp.broadcast_to(
        crowded(requests_ref[...], base, sends[-1].shape[0], subj_dev), ends_ref.shape[1:]
    )
    for o in range(spaces):
        used[o] = wanted_ref[me, COUNTS + o]
    for i, (code, valid) in enumerate(edge_codes(wanted_ref, me, subj_dev)):
        owner = jnp.where(valid, lax.shift_right_logical(code, SHIFT), 0)
        place = used[owner]
        edge_slots[i] = jnp.where(valid, lax.bitwise_xor(owner, me) * total + place, 0)
        used[owner] = place + jnp.where(valid, 1, 0)
    for copy in fetches:
        copy.wait()
    for side, (out, i) in enumerate(((sends[1], total), (side_ref, 0))):
        for c in range(3):
            for s in range(subj_dev):
                for r in range(EDGE):
                    out[i] = v_ref[side, c, s, r].astype(out.dtype)
                    out[i + 1] = w_ref[side, c, s, r]
                    i = i + 2


def pick(answers, images, template, velocity, weights, cap, sizes):
    spaces = answers.shape[0]
    subj_dev = velocity.shape[1]
    total = cap + 2 * EDGE * subj_dev
    tile = images.shape[1:]
    packed = 2 * EDGE * 3 * subj_dev
    base = sizes.index(min(sizes))
    longer = [n + packed if k == 1 else n for k, n in enumerate(sizes)]
    outs = [shaped((n,) + tile, images.dtype) for n in longer]
    outs += [shaped((total - n,) + tile, images.dtype) for n in sizes[base:]]
    got = pl.pallas_call(
        functools.partial(pick_kernel, cap, base, total),
        out_shape=outs
        + [
            shaped((2 * EDGE * subj_dev,), jnp.int32),
            shaped((packed,) + tile, images.dtype),
            shaped((template.shape[0] + 2 * EDGE + 1,) + template.shape[1:]),
        ],
        in_specs=[VMEM, VMEM, ANY, ANY, ANY],
        out_specs=[VMEM] * len(outs) + [SMEM, VMEM, VMEM],
        scratch_shapes=[
            pltpu.VMEM((spaces, LANES), jnp.int32),
            pltpu.SMEM((spaces, LANES), jnp.int32),
            pltpu.SMEM((spaces,), jnp.int32),
            pltpu.VMEM((2, 3, subj_dev, EDGE) + tile, velocity.dtype),
            pltpu.VMEM((2, 3, subj_dev, EDGE) + tile, weights.dtype),
            pltpu.SemaphoreType.DMA((6,)),
        ],
        compiler_params=params(),
        name="pick",
    )(answers, images, *map(in_hbm, (template, velocity, weights)))
    return got[:spaces], got[spaces:-3], *got[-3:]


def up_x(v):
    return pltpu.roll(v, v.shape[0] - BY, 0)


def up_y(v):
    return pltpu.roll(v, v.shape[0] - 1, 0)


def up_z(v):
    return pltpu.roll(v, v.shape[1] - 1, 1)


def down_x(v):
    return pltpu.roll(v, BY, 0)


def down_y(v):
    return pltpu.roll(v, 1, 0)


def down_z(v):
    return pltpu.roll(v, 1, 1)


def inside(shape, value):
    p = lax.broadcasted_iota(jnp.int32, shape, 0)
    z = lax.broadcasted_iota(jnp.int32, shape, 1)
    y = lax.bitwise_and(p, BY - 1)
    conditions = (
        p < shape[0] - BY,
        p >= BY,
        y < BY - 1,
        y > 0,
        z < shape[1] - 1,
        z > 0,
    )
    return [jnp.where(c, value, 0.0).astype(jnp.float32) for c in conditions]


def warp_tile(brick, fractions, masks, live):
    frac_x, frac_y, frac_z = (f.astype(jnp.float32) for f in fractions)
    high_x, high_y, high_z = frac_x * masks[0], frac_y * masks[2], frac_z * masks[4]
    low_x, low_y, low_z = 1.0 - frac_x, 1.0 - frac_y, 1.0 - frac_z
    low_x, high_x = low_x * live, high_x * live

    def along_z(v):
        return low_z * v + high_z * up_z(v)

    def along_y(v):
        return low_y * along_z(v) + high_y * along_z(up_y(v))

    return low_x * along_y(brick) + high_x * along_y(up_x(brick))


def slopes(w, halves):
    return (
        up_x(w) * halves[0] - down_x(w) * halves[1],
        up_y(w) * halves[2] - down_y(w) * halves[3],
        up_z(w) * halves[4] - down_z(w) * halves[5],
    )


def predict(w, g, f):
    return w + (g[0] * f[0] + g[1] * f[1]) + g[2] * f[2]


def smooth(before, here, after, masks):
    rowwise = (before + after) + (here + here)
    return (down_z(rowwise) * masks[5] + up_z(rowwise) * masks[4]) + (rowwise + rowwise)


def first_kernel(spaces, base, groups, *refs):
    counts_ref, slots_ref, edge_slots_ref = refs[:3]
    parts, refs = refs[3 : 3 + spaces], refs[3 + spaces :]
    overs, refs = refs[: spaces - base], refs[spaces - base :]
    shares, refs = refs[:groups], refs[groups:]
    side_ref, weights_in, velocity_in = refs[:3]
    warped_ref, slopes_ref, scale_ref, field_ref, keep_ref, send_ref = refs[3:9]
    table, update, weights_ref, packs, chunk_sems = refs[9:]
    _, subj_dev, rows, plane, depth = weights_ref.shape
    total = parts[0].shape[0]
    short = parts[-1].shape[0]
    cap = total - 2 * EDGE * subj_dev
    me, position = lax.axis_index("space"), lax.axis_index("subj")
    core = lax.bitwise_and(position, 1)
    odd = lax.bitwise_and(me, 1)
    chunks = chunk_sems.shape[0] // 2
    chunk = rows // chunks
    chunk_copies = []
    for i in range(chunks):
        part = pl.ds(i * chunk, chunk)
        chunk_copies.append(
            [
                pltpu.make_async_copy(source.at[:, :, part], target, chunk_sems.at[n])
                for n, source, target in (
                    (2 * i, weights_in, weights_ref.at[:, :, part]),
                    (2 * i + 1, velocity_in, field_ref.at[:, :, pl.ds(1 + i * chunk, chunk)]),
                )
            ]
        )
    for copy in sum(chunk_copies, []):
        copy.start()
    for k in range(spaces):
        for c in range(total):
            if k < base or c < short:
                table[k * total + c] = parts[k][c]
            else:
                table[k * total + c] = overs[k - base][c - short]
    for i in range(packs.shape[1]):
        packs[1 - odd, i] = parts[1][total + i]
        packs[odd, i] = side_ref[i]
    before_ref, after_ref = packs.at[0], packs.at[1]
    masks, halves = inside((plane, depth), 1.0), inside((plane, depth), 0.5)

    def tile(s, e, brick, fractions, live, f, current):
        w = warp_tile(brick.astype(jnp.float32), fractions, masks, live)
        g = slopes(w, halves)
        scale = 0.0625 / (g[0] * g[0] + g[1] * g[1] + g[2] * g[2] + RIDGE)
        ratio = (predict(w, g, f) - current) * scale
        warped_ref[s, e] = w
        scale_ref[s, e] = scale
        for c in range(3):
            slopes_ref[c, s, e] = g[c]
            update[c, s, e] = g[c] * ratio

    def template_row(r):
        parts = [shares[k][r] for k in range(groups)]
        mask = 1
        while mask < groups:
            turned = lax.bitwise_and(position, mask) > 0
            parts = [jnp.where(turned, parts[i ^ mask], part) for i, part in enumerate(parts)]
            mask = 2 * mask
        return jnp.concatenate(parts, axis=0)

    def row(r, carry):
        current = template_row(r)
        for s in range(subj_dev):
            count = counts_ref[0, s]
            first = lax.shift_right_logical(count, 1)
            alive = (r < first) | (r >= rows - (count - first))
            live = jnp.where(alive, 1.0, 0.0).astype(jnp.float32)
            wanted = slots_ref[s, r]
            owner = lax.div(wanted, cap)
            slot = lax.bitwise_xor(owner, me) * total + (wanted - owner * cap)
            tile(
                s,
                r + EDGE,
                table[slot],
                [weights_ref[c, s, r] for c in range(3)],
                live,
                [field_ref[c, s, r + 1] for c in range(3)],
                current,
            )
        return carry

    for side, (ref, there, e0) in enumerate(
        ((before_ref, me > 0, 0), (after_ref, me < spaces - 1, rows + EDGE))
    ):
        live = jnp.where(there, 1.0, 0.0).astype(jnp.float32)
        for r in range(EDGE):
            current = template_row(rows + side * EDGE + r)
            for s in range(subj_dev):
                at = [2 * ((c * subj_dev + s) * EDGE + r) for c in range(3)]
                tile(
                    s,
                    e0 + r,
                    table[edge_slots_ref[(side * subj_dev + s) * EDGE + r]],
                    [ref[a + 1] for a in at],
                    live,
                    [ref[a].astype(jnp.float32) for a in at],
                    current,
                )

    for i in range(chunks):
        for copy in chunk_copies[i]:
            copy.wait()
        lax.fori_loop(i * chunk, (i + 1) * chunk, row, 0, unroll=8)

    for c in range(3):
        for s in range(subj_dev):
            at = 2 * (c * subj_dev + s) * EDGE
            field_ref[c, s, 0] = before_ref[at + 2 * (EDGE - 1)].astype(jnp.float32)
            field_ref[c, s, rows + 1] = after_ref[at].astype(jnp.float32)

    def move(i, carry):
        e = i + EDGE - 1
        total_p = None
        for s in range(subj_dev):
            g = [slopes_ref[c, s, e] for c in range(3)]
            f = []
            for c in range(3):
                delta = smooth(update[c, s, e - 1], update[c, s, e], update[c, s, e + 1], masks)
                f.append(field_ref[c, s, i] - delta)
                field_ref[c, s, i] = f[c]
            p = predict(warped_ref[s, e], g, f)
            total_p = p if total_p is None else total_p + p
        half = plane // 2
        low, high = total_p[:half], total_p[half:]
        keep_ref[i] = jnp.where(core == 0, low, high)
        send_ref[i] = jnp.where(core == 0, high, low)
        return carry

    lax.fori_loop(0, rows + 2, move, 0, unroll=11)


def first(counts, slots, edge_slots, parts, overs, shares, side, weights, velocity):
    _, subj_dev, rows, plane, depth = velocity.shape
    spaces = len(parts)
    total = parts[0].shape[0]
    long = rows + 2 * EDGE
    sums = shaped((rows + 2, plane // 2, depth))
    arrays = [*parts, *overs, *shares, side]
    return pl.pallas_call(
        functools.partial(first_kernel, spaces, spaces - len(overs), len(shares)),
        out_shape=(
            shaped((subj_dev, long, plane, depth)),
            shaped((3, subj_dev, long, plane, depth)),
            shaped((subj_dev, long, plane, depth)),
            shaped((3, subj_dev, rows + 2, plane, depth)),
            sums,
            sums,
        ),
        in_specs=[SMEM] * 3 + [VMEM] * len(arrays) + [ANY] * 2,
        out_specs=(VMEM,) * 6,
        scratch_shapes=[
            pltpu.VMEM((spaces * total, plane, depth), weights.dtype),
            pltpu.VMEM((3, subj_dev, long, plane, depth), jnp.float32),
            pltpu.VMEM(weights.shape, weights.dtype),
            pltpu.VMEM((2,) + side.shape, side.dtype),
            pltpu.SemaphoreType.DMA((8,)),
        ],
        compiler_params=params(),
        name="first",
    )(counts, slots, edge_slots, *arrays, in_hbm(weights), in_hbm(velocity))


def last_kernel(
    mine_ref,
    other_ref,
    warped_ref,
    slopes_ref,
    scale_ref,
    field_ref,
    out_ref,
    keep_ref,
    send_ref,
    update,
    out,
    sems,
):
    _, subj_dev, rows, plane, depth = out.shape
    core = lax.bitwise_and(lax.axis_index("subj"), 1)
    masks = inside((plane, depth), 1.0)
    chunks = sems.shape[0]
    chunk = rows // chunks

    def renew(i, carry):
        mine, other = mine_ref[i].astype(jnp.float32), other_ref[i].astype(jnp.float32)
        current = jnp.concatenate(
            [jnp.where(core == 0, mine, other), jnp.where(core == 0, other, mine)], axis=0
        )
        for s in range(subj_dev):
            g = [slopes_ref[c, s, i + 1] for c in range(3)]
            f = [field_ref[c, s, i] for c in range(3)]
            ratio = (predict(warped_ref[s, i + 1], g, f) - current) * scale_ref[s, i + 1]
            for c in range(3):
                update[c, s, i] = g[c] * ratio
        return carry

    lax.fori_loop(0, rows + 2, renew, 0, unroll=11)

    def move(r, carry):
        total = None
        for s in range(subj_dev):
            g = [slopes_ref[c, s, r + EDGE] for c in range(3)]
            f = []
            for c in range(3):
                delta = smooth(update[c, s, r], update[c, s, r + 1], update[c, s, r + 2], masks)
                f.append(field_ref[c, s, r + 1] - delta)
                out[c, s, r] = f[c]
            p = predict(warped_ref[s, r + EDGE], g, f)
            total = p if total is None else total + p
        quarter = plane // 4
        low, high = total[: 2 * quarter], total[2 * quarter :]
        upper = lax.broadcasted_iota(jnp.int32, low.shape, 0) >= quarter
        even = jnp.where(upper, pltpu.roll(high, quarter, 0), low)
        odd = jnp.where(upper, high, pltpu.roll(low, quarter, 0))
        keep_ref[r] = jnp.where(core == 0, even, odd)
        send_ref[r] = jnp.where(core == 0, odd, even)
        return carry

    copies = []
    for i in range(chunks):
        lax.fori_loop(i * chunk, (i + 1) * chunk, move, 0, unroll=16)
        part = pl.ds(i * chunk, chunk)
        copy = pltpu.make_async_copy(out.at[:, :, part], out_ref.at[:, :, part], sems.at[i])
        copy.start()
        copies.append(copy)
    for copy in copies:
        copy.wait()


def last(mine, other, warped, slopes_all, scale, field, rows):
    _, subj_dev, _, plane, depth = field.shape
    shape = (3, subj_dev, rows, plane, depth)
    sums = shaped((rows, plane // 2, depth))
    return pl.pallas_call(
        last_kernel,
        out_shape=(shaped(shape), sums, sums),
        in_specs=[VMEM] * 6,
        out_specs=(ANY, VMEM, VMEM),
        scratch_shapes=[
            pltpu.VMEM(field.shape, jnp.float32),
            pltpu.VMEM(shape, jnp.float32),
            pltpu.SemaphoreType.DMA((4,)),
        ],
        compiler_params=params(),
        name="last",
    )(mine, other, warped, slopes_all, scale, field)


def fold_kernel(keep_ref, got_ref, own_ref, away_ref):
    second = lax.shift_right_logical(lax.axis_index("subj"), 1) == 1
    quarter = own_ref.shape[1]

    def row(r, carry):
        total = keep_ref[r] + got_ref[r]
        low, high = total[:quarter], total[quarter:]
        own_ref[r] = jnp.where(second, high, low)
        away_ref[r] = jnp.where(second, low, high)
        return carry

    lax.fori_loop(0, keep_ref.shape[0], row, 0, unroll=8)


def fold(keep, got):
    rows, half, depth = keep.shape
    part = shaped((rows, half // 2, depth))
    return pl.pallas_call(
        fold_kernel,
        out_shape=(part, part),
        in_specs=[VMEM] * 2,
        out_specs=(VMEM,) * 2,
        compiler_params=params(),
        name="fold",
    )(keep, got)


def swap(value, axis, mask):
    count = lax.axis_size(axis)
    return lax.ppermute(value, axis, [(i, i ^ mask) for i in range(count)])


def body(images, velocity, weights, template, owners, local_rows, tile_counts):
    spaces = lax.axis_size("space")
    groups = lax.axis_size("subj")
    subj_dev, rows, plane, depth = images.shape
    cap = subj_dev * (2 * rows // spaces)
    subjects = subj_dev * groups
    counts = jnp.swapaxes(tile_counts, 0, 1)

    request, slots, held = plan(
        counts,
        jnp.swapaxes(owners, 1, 2),
        local_rows,
        images.reshape(subj_dev * rows, plane, depth),
        template,
        cap,
        spaces,
    )
    answers = lax.all_to_all(request, "space", split_axis=0, concat_axis=0, tiled=True)

    base = spaces // 2
    total = cap + 2 * EDGE * subj_dev
    short = cap - cap // 8
    sizes = [total] * base + [short] * (spaces - base)
    sends, overs, edge_slots, side, ends = pick(
        answers, held, template, velocity, weights, cap, sizes
    )
    far = [swap(sends[k], "space", k) for k in range(base, spaces)]
    shares = [ends] + [swap(ends, "subj", k) for k in range(1, groups)]
    near = [sends[0]] + [swap(sends[k], "space", k) for k in range(1, base)]
    others = [(i, i + 1) for i in range(1, spaces - 1, 2)]
    side = lax.ppermute(side, "space", others + [(j, i) for i, j in others])
    over = functools.reduce(jnp.maximum, [share[-1, 0, 0] for share in shares])
    overs = list(overs)
    overs, far, near[1:], side = lax.optimization_barrier((overs, far, near[1:], side))
    def again(state):
        parts = [swap(part, "space", base + i) for i, part in enumerate(state[1])]
        return 0.0, parts

    _, overs = lax.while_loop(lambda state: state[0] > 0, again, (over, overs))

    warped, slopes_all, scale, field, keep, send = first(
        counts, slots, edge_slots, near + far, overs, shares, side, weights, velocity
    )
    share = keep + swap(send, "subj", 1)
    mask = 2
    while mask < groups:
        share = share + swap(share.astype(jnp.bfloat16), "subj", mask).astype(jnp.float32)
        mask = 2 * mask
    mine = (share / subjects).astype(jnp.bfloat16)
    other = swap(mine, "subj", 1)

    field, keep, send = last(mine, other, warped, slopes_all, scale, field, rows)
    if groups == 4:
        own, away = fold(keep, swap(send, "subj", 1))
        result = (own + swap(away, "subj", 2)) / subjects
    else:
        quarter = plane // 4
        core = lax.bitwise_and(lax.axis_index("subj"), 1)
        even = jnp.where(core == 0, keep, send)
        odd = jnp.where(core == 0, send, keep)
        full = jnp.concatenate(
            [even[:, :quarter], odd[:, :quarter], even[:, quarter:], odd[:, quarter:]], axis=1
        )
        result = lax.psum_scatter(full, "subj", scatter_dimension=1, tiled=True) / subjects
    return field, result


def solution(mesh):
    in_specs = (
        P("subj", "space", None, None),
        P(None, "subj", "space", None, None),
        P(None, "subj", "space", None, None),
        P("space", "subj", None),
        P("subj", "space", None),
        P("subj", "space"),
        P("subj", "space"),
    )
    out_specs = (P(None, "subj", "space", None, None), P("space", "subj", None))
    return jax.shard_map(body, mesh=mesh, in_specs=in_specs, out_specs=out_specs, check_vma=False)
```

```python
import functools

import jax
import jax.numpy as jnp
from jax import lax
from jax.experimental import pallas as pl
from jax.experimental.pallas import tpu as pltpu
from jax.sharding import PartitionSpec as P

BY = 4
ITERS = 2
RIDGE = 0.25
LANES = 128
LIMIT = 24 * 1024 * 1024
EDGE = 2
CODES = 48
COUNTS = 64
SHIFT = 8

VMEM = pl.BlockSpec(memory_space=pltpu.VMEM)
SMEM = pl.BlockSpec(memory_space=pltpu.SMEM)
ANY = pl.BlockSpec(memory_space=pl.ANY)
SMALL = pl.CostEstimate(flops=0, bytes_accessed=0, transcendentals=0)


def params():
    return pltpu.CompilerParams(vmem_limit_bytes=LIMIT)


def shaped(shape, dtype=jnp.float32):
    return jax.ShapeDtypeStruct(shape, dtype)


def in_hbm(value):
    return pltpu.with_memory_space_constraint(value, pltpu.HBM)


def in_vmem(value):
    return pltpu.with_memory_space_constraint(value, pltpu.VMEM)


def plan_kernel(
    cap,
    counts_in,
    owners_in,
    rows_in,
    images_ref,
    velocity_ref,
    weights_ref,
    request_ref,
    slots_ref,
    held_ref,
    near_ref,
    side_ref,
    counts_ref,
    owners_ref,
    rows_ref,
    v_ref,
    w_ref,
    sems,
):
    subj_dev, rows = rows_ref.shape
    spaces = request_ref.shape[0]
    odd = lax.bitwise_and(lax.axis_index("space"), 1)
    copies = [
        pltpu.make_async_copy(source, target, sems.at[i])
        for i, (source, target) in enumerate(
            (
                (counts_in, counts_ref),
                (owners_in, owners_ref),
                (rows_in, rows_ref),
                (images_ref, held_ref),
                (velocity_ref.at[:, :, pl.ds(0, EDGE)], v_ref.at[1 - odd]),
                (weights_ref.at[:, :, pl.ds(0, EDGE)], w_ref.at[1 - odd]),
                (velocity_ref.at[:, :, pl.ds(rows - EDGE, EDGE)], v_ref.at[odd]),
                (weights_ref.at[:, :, pl.ds(rows - EDGE, EDGE)], w_ref.at[odd]),
            )
        )
    ]
    for copy in copies:
        copy.start()
    for copy in copies[:3]:
        copy.wait()
    t = lax.broadcasted_iota(jnp.int32, (rows, rows), 0)
    u = lax.broadcasted_iota(jnp.int32, (rows, rows), 1)
    eye = t == u
    lane = lax.broadcasted_iota(jnp.int32, (rows, LANES), 1)
    line = lax.broadcasted_iota(jnp.int32, (1, LANES), 1)
    sub = lax.broadcasted_iota(jnp.int32, (spaces, LANES), 0)
    zero = jnp.zeros((rows, rows), jnp.int32)
    request = jnp.zeros((spaces, LANES), jnp.int32)
    extra = jnp.zeros((1, LANES), jnp.int32)
    earlier_subjects = []
    for s in range(subj_dev):
        count = counts_ref[0, s]
        first = lax.shift_right_logical(count, 1)
        owner_u = jnp.broadcast_to(owners_ref[s], (rows, rows))
        row_u = jnp.broadcast_to(rows_ref[s : s + 1, :], (rows, rows))
        owner_t = jnp.broadcast_to(
            jnp.sum(jnp.where(eye, owner_u, zero), axis=1, keepdims=True), (rows, rows)
        )
        row_t = jnp.broadcast_to(
            jnp.sum(jnp.where(eye, row_u, zero), axis=1, keepdims=True), (rows, rows)
        )
        last = rows - (count - first)
        alive_t = (t < first) | (t >= last)
        alive_u = (u < first) | (u >= last)
        same_owner = owner_t == owner_u
        same = same_owner & (row_t == row_u)
        dup_u = jnp.sum(jnp.where(same & alive_t & (t < u), 1, 0), axis=0, keepdims=True)
        dup_t = jnp.sum(jnp.where(same & alive_u & (u < t), 1, 0), axis=1, keepdims=True)
        first_u = alive_u & jnp.broadcast_to(dup_u == 0, (rows, rows))
        first_t = alive_t & jnp.broadcast_to(dup_t == 0, (rows, rows))
        place = jnp.sum(jnp.where(same_owner & first_u & (u < t), 1, 0), axis=1, keepdims=True)
        for owner_v, first_v in earlier_subjects:
            place = place + jnp.sum(
                jnp.where((owner_t == owner_v) & first_v, 1, 0), axis=1, keepdims=True
            )
        earlier_subjects.append((owner_u, first_u))
        slot_t = owner_t * cap + place
        slots_ref[s : s + 1, :] = jnp.sum(
            jnp.where(same & first_t & alive_u, slot_t, zero), axis=0, keepdims=True
        )
        wide_first = jnp.broadcast_to(first_t[:, :1], (rows, LANES))
        wide_owner = jnp.broadcast_to(owner_t[:, :1], (rows, LANES))
        wide_place = jnp.broadcast_to(place, (rows, LANES))
        wide_row = jnp.broadcast_to(row_t[:, :1], (rows, LANES)) + s * rows
        wide_tile = lax.broadcasted_iota(jnp.int32, (rows, LANES), 0)
        hit = jnp.where(wide_first & (wide_place == lane), wide_row, 0)
        for o in range(spaces):
            asked = jnp.sum(jnp.where(wide_owner == o, hit, 0), axis=0, keepdims=True)
            request = request + jnp.where(sub == o, asked, 0)
        counted = jnp.where(wide_first & (wide_owner == lane - COUNTS), 1, 0)
        extra = extra + jnp.sum(counted, axis=0, keepdims=True)
        for side, begin in enumerate((0, rows - EDGE)):
            place = CODES + (side * subj_dev + s) * EDGE
            code = jnp.where(
                wide_tile - begin == lane - place, lax.shift_left(wide_owner, SHIFT) + wide_row, 0
            )
            code = jnp.sum(code, axis=0, keepdims=True)
            extra = extra + jnp.where((line >= place) & (line < place + EDGE), code, 0)
    request_ref[...] = request + jnp.broadcast_to(extra, request.shape)
    for copy in copies[3:]:
        copy.wait()
    for place, out in enumerate((near_ref, side_ref)):
        i = 0
        for c in range(3):
            for s in range(subj_dev):
                for r in range(EDGE):
                    out[i] = v_ref[place, c, s, r].astype(out.dtype)
                    out[i + 1] = w_ref[place, c, s, r]
                    i = i + 2


def plan(counts, owners, local_rows, images, velocity, weights, cap, spaces):
    subj_dev, rows = local_rows.shape
    tile = velocity.shape[3:]
    edge = shaped((2 * EDGE * 3 * subj_dev,) + tile, weights.dtype)
    return pl.pallas_call(
        functools.partial(plan_kernel, cap),
        out_shape=(
            shaped((spaces, LANES), jnp.int32),
            shaped((subj_dev, rows), jnp.int32),
            pltpu.VMEM(images.shape, images.dtype),
            edge,
            edge,
        ),
        in_specs=[ANY] * 6,
        out_specs=(VMEM,) * 5,
        scratch_shapes=[
            pltpu.SMEM(counts.shape, jnp.int32),
            pltpu.VMEM(owners.shape, jnp.int32),
            pltpu.VMEM(local_rows.shape, jnp.int32),
            pltpu.VMEM((2, 3, subj_dev, EDGE) + tile, velocity.dtype),
            pltpu.VMEM((2, 3, subj_dev, EDGE) + tile, weights.dtype),
            pltpu.SemaphoreType.DMA((8,)),
        ],
        compiler_params=params(),
        name="plan",
    )(*map(in_hbm, (counts, owners, local_rows, images, velocity, weights)))


def edge_codes(wanted_ref, me, subj_dev):
    spaces = wanted_ref.shape[0]
    before, after = jnp.maximum(me - 1, 0), jnp.minimum(me + 1, spaces - 1)
    found = []
    for i in range(subj_dev * EDGE):
        found.append((wanted_ref[before, CODES + subj_dev * EDGE + i], me > 0))
    for i in range(subj_dev * EDGE):
        found.append((wanted_ref[after, CODES + i], me < spaces - 1))
    return found


def crowded(wanted, base, size, subj_dev):
    spaces, lanes = wanted.shape
    d = lax.broadcasted_iota(jnp.int32, (spaces, lanes), 0)
    owner = lax.broadcasted_iota(jnp.int32, (spaces, lanes), 1) - COUNTS
    need = wanted
    for side in range(2):
        codes = pltpu.roll(wanted, 1 if side == 0 else spaces - 1, 0)
        valid = d > 0 if side == 0 else d < spaces - 1
        begin = CODES + (subj_dev * EDGE if side == 0 else 0)
        for i in range(subj_dev * EDGE):
            code = jnp.broadcast_to(codes[:, begin + i : begin + i + 1], (spaces, lanes))
            hit = valid & (lax.shift_right_logical(code, SHIFT) == owner)
            need = need + jnp.where(hit, 1, 0)
    pair = (owner >= 0) & (owner < spaces) & (lax.bitwise_xor(owner, d) >= base)
    over = jnp.where(pair & (need > size), 1.0, 0.0)
    return jnp.max(jnp.max(over, axis=0, keepdims=True), axis=1, keepdims=True)


def whole_row(shares, r, position):
    parts = [share[r] for share in shares]
    mask = 1
    while mask < len(shares):
        turned = lax.bitwise_and(position, mask) > 0
        parts = [jnp.where(turned, parts[i ^ mask], part) for i, part in enumerate(parts)]
        mask = 2 * mask
    return jnp.concatenate(parts, axis=0)


def carries(spaces):
    return [k for k in range(3, spaces) if k & (k + 1) == 0]


def pick_kernel(cap, base, total, groups, wanted_ref, requests_ref, images_ref, near_ref, *refs):
    shares, refs = refs[:groups], refs[groups + 1 :]
    spaces = requests_ref.shape[0]
    sends, overs = refs[:spaces], refs[spaces : 2 * spaces - base]
    edge_slots, over_ref, used = refs[-3:]
    rows = shares[0].shape[0]
    subj_dev = (total - cap) // (2 * EDGE)
    me, position = lax.axis_index("space"), lax.axis_index("subj")
    odd = lax.bitwise_and(me, 1)
    short = sends[-1].shape[0] - 2 * EDGE
    for k in range(spaces):
        target = lax.bitwise_xor(me, k)
        size = short if k >= base else total

        def put(c, brick, k=k, size=size):
            if isinstance(c, int):
                ref, c = (sends[k], c) if c < size else (overs[k - base], c - size)
                ref[c] = brick
            elif k < base:
                sends[k][c] = brick
            else:

                @pl.when(c < size)
                def _():
                    sends[k][c] = brick

                @pl.when(c >= size)
                def _():
                    overs[k - base][c - size] = brick

        for c in range(cap):
            put(c, images_ref[wanted_ref[target, c]])
        place = wanted_ref[target, COUNTS + me]
        for code, valid in edge_codes(wanted_ref, target, subj_dev):
            mine = valid & (lax.shift_right_logical(code, SHIFT) == me)

            @pl.when(mine)
            def _(code=code, place=place, put=put):
                put(place, images_ref[lax.bitwise_and(code, (1 << SHIFT) - 1)])

            place = place + jnp.where(mine, 1, 0)
    over_ref[0] = jnp.max(crowded(requests_ref[...], base, short, subj_dev)).astype(jnp.int32)
    for o in range(spaces):
        used[o] = wanted_ref[me, COUNTS + o]
    for i, (code, valid) in enumerate(edge_codes(wanted_ref, me, subj_dev)):
        owner = jnp.where(valid, lax.shift_right_logical(code, SHIFT), 0)
        place = used[owner]
        edge_slots[i] = jnp.where(valid, lax.bitwise_xor(owner, me) * total + place, 0)
        used[owner] = place + jnp.where(valid, 1, 0)
    for i in range(near_ref.shape[0]):
        sends[1][total + 2 * EDGE + i] = near_ref[i]
    for r in range(EDGE):
        low = whole_row(shares, r, position)
        high = whole_row(shares, rows - EDGE + r, position)
        for k in [1, *carries(spaces)]:
            value = jnp.where((odd == 1) == (k == 1), low, high)
            at = (short if k >= base else total) + 2 * r
            rounded = value.astype(sends[k].dtype)
            sends[k][at] = rounded
            sends[k][at + 1] = (value - rounded.astype(jnp.float32)).astype(sends[k].dtype)


def pick(wanted, images, near, shares, side, cap, sizes):
    spaces = wanted.shape[0]
    base = sizes.index(min(sizes))
    total = sizes[0]
    tile = images.shape[1:]
    longer = [n + 2 * EDGE * (k == 1 or k in carries(spaces)) for k, n in enumerate(sizes)]
    longer[1] += near.shape[0]
    outs = [shaped((n,) + tile, images.dtype) for n in longer]
    outs += [shaped((total - n,) + tile, images.dtype) for n in sizes[base:]]
    edges = total - cap
    got = pl.pallas_call(
        functools.partial(pick_kernel, cap, base, total, len(shares)),
        out_shape=outs + [shaped((edges,), jnp.int32), shaped((1,), jnp.int32)],
        in_specs=[SMEM] + [VMEM] * (3 + len(shares)) + [ANY],
        out_specs=[VMEM] * len(outs) + [SMEM, SMEM],
        scratch_shapes=[pltpu.SMEM((spaces,), jnp.int32)],
        compiler_params=params(),
        name="pick",
    )(wanted, wanted, images, near, *shares, side)
    return got[:spaces], got[spaces:-2], *got[-2:]


def up_x(v):
    return pltpu.roll(v, v.shape[0] - BY, 0)


def up_y(v):
    return pltpu.roll(v, v.shape[0] - 1, 0)


def up_z(v):
    return pltpu.roll(v, v.shape[1] - 1, 1)


def down_x(v):
    return pltpu.roll(v, BY, 0)


def down_y(v):
    return pltpu.roll(v, 1, 0)


def down_z(v):
    return pltpu.roll(v, 1, 1)


def inside(shape, value):
    p = lax.broadcasted_iota(jnp.int32, shape, 0)
    z = lax.broadcasted_iota(jnp.int32, shape, 1)
    y = lax.bitwise_and(p, BY - 1)
    conditions = (
        p < shape[0] - BY,
        p >= BY,
        y < BY - 1,
        y > 0,
        z < shape[1] - 1,
        z > 0,
    )
    return [jnp.where(c, value, 0.0).astype(jnp.float32) for c in conditions]


def warp_tile(brick, fractions, masks, live):
    frac_x, frac_y, frac_z = (f.astype(jnp.float32) for f in fractions)
    high_x, high_y, high_z = frac_x * masks[0], frac_y * masks[2], frac_z * masks[4]
    low_x, low_y, low_z = 1.0 - frac_x, 1.0 - frac_y, 1.0 - frac_z
    low_x, high_x = low_x * live, high_x * live

    def along_z(v):
        return low_z * v + high_z * up_z(v)

    def along_y(v):
        return low_y * along_z(v) + high_y * along_z(up_y(v))

    return low_x * along_y(brick) + high_x * along_y(up_x(brick))


def slopes(w, halves):
    return (
        up_x(w) * halves[0] - down_x(w) * halves[1],
        up_y(w) * halves[2] - down_y(w) * halves[3],
        up_z(w) * halves[4] - down_z(w) * halves[5],
    )


def predict(w, g, f):
    return w + (g[0] * f[0] + g[1] * f[1]) + g[2] * f[2]


def smooth(before, here, after, masks):
    rowwise = (before + after) + (here + here)
    return (down_z(rowwise) * masks[5] + up_z(rowwise) * masks[4]) + (rowwise + rowwise)


def first_kernel(spaces, base, groups, *refs):
    counts_ref, slots_ref, edge_slots_ref = refs[:3]
    parts, refs = refs[3 : 3 + spaces], refs[3 + spaces :]
    overs, refs = refs[: spaces - base], refs[spaces - base :]
    shares, refs = refs[:groups], refs[groups:]
    side_ref, weights_in, velocity_in = refs[:3]
    warped_ref, slopes_ref, scale_ref, field_ref, keep_ref, send_ref = refs[3:9]
    table, update, weights_ref, packs, chunk_sems = refs[9:]
    _, subj_dev, rows, plane, depth = weights_ref.shape
    total = parts[0].shape[0]
    short = parts[-1].shape[0] - 2 * EDGE
    cap = total - 2 * EDGE * subj_dev
    me, position = lax.axis_index("space"), lax.axis_index("subj")
    core = lax.bitwise_and(position, 1)
    odd = lax.bitwise_and(me, 1)
    chunks = chunk_sems.shape[0] // 2
    chunk = rows // chunks
    chunk_copies = []
    for i in range(chunks):
        part = pl.ds(i * chunk, chunk)
        chunk_copies.append(
            [
                pltpu.make_async_copy(source.at[:, :, part], target, chunk_sems.at[n])
                for n, source, target in (
                    (2 * i, weights_in, weights_ref.at[:, :, part]),
                    (2 * i + 1, velocity_in, field_ref.at[:, :, pl.ds(1 + i * chunk, chunk)]),
                )
            ]
        )
    for copy in sum(chunk_copies, []):
        copy.start()
    for k in range(spaces):
        for c in range(total):
            if k < base or c < short:
                table[k * total + c] = parts[k][c]
            else:
                table[k * total + c] = overs[k - base][c - short]
    for i in range(side_ref.shape[0]):
        packs[1 - odd, 2 * EDGE + i] = parts[1][total + 2 * EDGE + i]
        packs[odd, 2 * EDGE + i] = side_ref[i]
    for i in range(2 * EDGE):
        packs[1 - odd, i] = parts[1][total + i]
        packs[odd, i] = jnp.zeros_like(side_ref[0])
    other = lax.bitwise_xor(me, me - 1 + 2 * odd)
    for k in carries(spaces):

        @pl.when(other == k)
        def _(k=k):
            for i in range(2 * EDGE):
                packs[odd, i] = parts[k][(short if k >= base else total) + i]

    before_ref, after_ref = packs.at[0], packs.at[1]
    masks, halves = inside((plane, depth), 1.0), inside((plane, depth), 0.5)

    def tile(s, e, brick, fractions, live, f, current):
        w = warp_tile(brick.astype(jnp.float32), fractions, masks, live)
        g = slopes(w, halves)
        scale = 0.0625 / (g[0] * g[0] + g[1] * g[1] + g[2] * g[2] + RIDGE)
        ratio = (predict(w, g, f) - current) * scale
        warped_ref[s, e] = w
        scale_ref[s, e] = scale
        for c in range(3):
            slopes_ref[c, s, e] = g[c]
            update[c, s, e] = g[c] * ratio

    def row(r, carry):
        current = whole_row(shares, r, position)
        for s in range(subj_dev):
            count = counts_ref[0, s]
            first = lax.shift_right_logical(count, 1)
            alive = (r < first) | (r >= rows - (count - first))
            live = jnp.where(alive, 1.0, 0.0).astype(jnp.float32)
            wanted = slots_ref[s, r]
            owner = lax.div(wanted, cap)
            slot = lax.bitwise_xor(owner, me) * total + (wanted - owner * cap)
            tile(
                s,
                r + EDGE,
                table[slot],
                [weights_ref[c, s, r] for c in range(3)],
                live,
                [field_ref[c, s, r + 1] for c in range(3)],
                current,
            )
        return carry

    for side, (ref, there, e0) in enumerate(
        ((before_ref, me > 0, 0), (after_ref, me < spaces - 1, rows + EDGE))
    ):
        live = jnp.where(there, 1.0, 0.0).astype(jnp.float32)
        for r in range(EDGE):
            current = ref[2 * r].astype(jnp.float32) + ref[2 * r + 1].astype(jnp.float32)
            for s in range(subj_dev):
                at = [2 * ((c * subj_dev + s + 1) * EDGE + r) for c in range(3)]
                tile(
                    s,
                    e0 + r,
                    table[edge_slots_ref[(side * subj_dev + s) * EDGE + r]],
                    [ref[a + 1] for a in at],
                    live,
                    [ref[a].astype(jnp.float32) for a in at],
                    current,
                )

    for i in range(chunks):
        for copy in chunk_copies[i]:
            copy.wait()
        lax.fori_loop(i * chunk, (i + 1) * chunk, row, 0, unroll=8)

    for c in range(3):
        for s in range(subj_dev):
            at = 2 * (c * subj_dev + s + 1) * EDGE
            field_ref[c, s, 0] = before_ref[at + 2 * (EDGE - 1)].astype(jnp.float32)
            field_ref[c, s, rows + 1] = after_ref[at].astype(jnp.float32)

    def move(i, carry):
        e = i + EDGE - 1
        total_p = None
        for s in range(subj_dev):
            g = [slopes_ref[c, s, e] for c in range(3)]
            f = []
            for c in range(3):
                delta = smooth(update[c, s, e - 1], update[c, s, e], update[c, s, e + 1], masks)
                f.append(field_ref[c, s, i] - delta)
                field_ref[c, s, i] = f[c]
            p = predict(warped_ref[s, e], g, f)
            total_p = p if total_p is None else total_p + p
        half = plane // 2
        low, high = total_p[:half], total_p[half:]
        keep_ref[i] = jnp.where(core == 0, low, high)
        send_ref[i] = jnp.where(core == 0, high, low)
        return carry

    lax.fori_loop(0, rows + 2, move, 0, unroll=11)


def first(counts, slots, edge_slots, parts, overs, shares, side, weights, velocity):
    _, subj_dev, rows, plane, depth = velocity.shape
    spaces = len(parts)
    total = parts[0].shape[0]
    long = rows + 2 * EDGE
    sums = shaped((rows + 2, plane // 2, depth))
    arrays = [*parts, *overs, *shares, side]
    return pl.pallas_call(
        functools.partial(first_kernel, spaces, spaces - len(overs), len(shares)),
        out_shape=(
            shaped((subj_dev, long, plane, depth)),
            shaped((3, subj_dev, long, plane, depth)),
            shaped((subj_dev, long, plane, depth)),
            shaped((3, subj_dev, rows + 2, plane, depth)),
            sums,
            sums,
        ),
        in_specs=[SMEM] * 3 + [VMEM] * len(arrays) + [ANY] * 2,
        out_specs=(VMEM,) * 6,
        scratch_shapes=[
            pltpu.VMEM((spaces * total, plane, depth), weights.dtype),
            pltpu.VMEM((3, subj_dev, long, plane, depth), jnp.float32),
            pltpu.VMEM(weights.shape, weights.dtype),
            pltpu.VMEM((2, side.shape[0] + 2 * EDGE) + side.shape[1:], side.dtype),
            pltpu.SemaphoreType.DMA((8,)),
        ],
        compiler_params=params(),
        name="first",
    )(counts, slots, edge_slots, *arrays, in_hbm(weights), in_hbm(velocity))


def last_kernel(
    mine_ref,
    other_ref,
    warped_ref,
    slopes_ref,
    scale_ref,
    field_ref,
    out_ref,
    keep_ref,
    send_ref,
    update,
    out,
    sems,
):
    _, subj_dev, rows, plane, depth = out.shape
    core = lax.bitwise_and(lax.axis_index("subj"), 1)
    masks = inside((plane, depth), 1.0)
    chunks = sems.shape[0]
    chunk = rows // chunks

    def renew(i, carry):
        mine, other = mine_ref[i].astype(jnp.float32), other_ref[i].astype(jnp.float32)
        current = jnp.concatenate(
            [jnp.where(core == 0, mine, other), jnp.where(core == 0, other, mine)], axis=0
        )
        for s in range(subj_dev):
            g = [slopes_ref[c, s, i + 1] for c in range(3)]
            f = [field_ref[c, s, i] for c in range(3)]
            ratio = (predict(warped_ref[s, i + 1], g, f) - current) * scale_ref[s, i + 1]
            for c in range(3):
                update[c, s, i] = g[c] * ratio
        return carry

    lax.fori_loop(0, rows + 2, renew, 0, unroll=11)

    def move(r, carry):
        total = None
        for s in range(subj_dev):
            g = [slopes_ref[c, s, r + EDGE] for c in range(3)]
            f = []
            for c in range(3):
                delta = smooth(update[c, s, r], update[c, s, r + 1], update[c, s, r + 2], masks)
                f.append(field_ref[c, s, r + 1] - delta)
                out[c, s, r] = f[c]
            p = predict(warped_ref[s, r + EDGE], g, f)
            total = p if total is None else total + p
        quarter = plane // 4
        low, high = total[: 2 * quarter], total[2 * quarter :]
        upper = lax.broadcasted_iota(jnp.int32, low.shape, 0) >= quarter
        even = jnp.where(upper, pltpu.roll(high, quarter, 0), low)
        odd = jnp.where(upper, high, pltpu.roll(low, quarter, 0))
        keep_ref[r] = jnp.where(core == 0, even, odd)
        send_ref[r] = jnp.where(core == 0, odd, even)
        return carry

    copies = []
    for i in range(chunks):
        lax.fori_loop(i * chunk, (i + 1) * chunk, move, 0, unroll=16)
        part = pl.ds(i * chunk, chunk)
        copy = pltpu.make_async_copy(out.at[:, :, part], out_ref.at[:, :, part], sems.at[i])
        copy.start()
        copies.append(copy)
    for copy in copies:
        copy.wait()


def last(mine, other, warped, slopes_all, scale, field, rows):
    _, subj_dev, _, plane, depth = field.shape
    shape = (3, subj_dev, rows, plane, depth)
    sums = shaped((rows, plane // 2, depth))
    return pl.pallas_call(
        last_kernel,
        out_shape=(shaped(shape), sums, sums),
        in_specs=[VMEM] * 6,
        out_specs=(ANY, VMEM, VMEM),
        scratch_shapes=[
            pltpu.VMEM(field.shape, jnp.float32),
            pltpu.VMEM(shape, jnp.float32),
            pltpu.SemaphoreType.DMA((4,)),
        ],
        compiler_params=params(),
        name="last",
    )(mine, other, warped, slopes_all, scale, field)


def fold_kernel(keep_ref, got_ref, own_ref, away_ref):
    second = lax.shift_right_logical(lax.axis_index("subj"), 1) == 1
    quarter = own_ref.shape[1]

    def row(r, carry):
        total = keep_ref[r] + got_ref[r]
        low, high = total[:quarter], total[quarter:]
        own_ref[r] = jnp.where(second, high, low)
        away_ref[r] = jnp.where(second, low, high)
        return carry

    lax.fori_loop(0, keep_ref.shape[0], row, 0, unroll=8)


def fold(keep, got):
    rows, half, depth = keep.shape
    part = shaped((rows, half // 2, depth))
    return pl.pallas_call(
        fold_kernel,
        out_shape=(part, part),
        in_specs=[VMEM] * 2,
        out_specs=(VMEM,) * 2,
        compiler_params=params(),
        name="fold",
    )(keep, got)


def swap(value, axis, mask):
    count = lax.axis_size(axis)
    return lax.ppermute(value, axis, [(i, i ^ mask) for i in range(count)])


def body(images, velocity, weights, template, owners, local_rows, tile_counts):
    spaces = lax.axis_size("space")
    groups = lax.axis_size("subj")
    subj_dev, rows, plane, depth = images.shape
    cap = subj_dev * (2 * rows // spaces)
    subjects = subj_dev * groups
    counts = jnp.swapaxes(tile_counts, 0, 1)

    request, slots, held, near_pack, side = plan(
        counts,
        jnp.swapaxes(owners, 1, 2),
        local_rows,
        images.reshape(subj_dev * rows, plane, depth),
        velocity,
        weights,
        cap,
        spaces,
    )
    others = [(i, i + 1) for i in range(1, spaces - 1, 2)]
    side = lax.ppermute(side, "space", others + [(j, i) for i, j in others])
    shares = [template] + [swap(template, "subj", k) for k in range(1, groups)]
    wanted = lax.all_to_all(request, "space", split_axis=0, concat_axis=0, tiled=True)

    base = spaces // 2
    total = cap + 2 * EDGE * subj_dev
    short = cap - cap // 8
    sizes = [total] * base + [short] * (spaces - base)
    sends, overs, edge_slots, over = pick(wanted, held, near_pack, shares, side, cap, sizes)
    far = [swap(sends[k], "space", k) for k in range(base, spaces)]
    near = [sends[0]] + [swap(sends[k], "space", k) for k in range(1, base)]

    def again(state):
        parts = [swap(part, "space", base + i) for i, part in enumerate(state[1])]
        return jnp.int32(0), parts

    _, overs = lax.while_loop(lambda state: state[0] > 0, again, (over[0], list(overs)))

    warped, slopes_all, scale, field, keep, send = first(
        counts, slots, edge_slots, near + far, overs, shares, side, weights, velocity
    )
    share = keep + swap(send, "subj", 1)
    mask = 2
    while mask < groups:
        share = share + swap(share.astype(jnp.bfloat16), "subj", mask).astype(jnp.float32)
        mask = 2 * mask
    mine = (share / subjects).astype(jnp.bfloat16)
    other = swap(mine, "subj", 1)

    field, keep, send = last(mine, other, warped, slopes_all, scale, field, rows)
    if groups == 4:
        own, away = fold(keep, swap(send, "subj", 1))
        result = (own + swap(away, "subj", 2)) / subjects
    else:
        quarter = plane // 4
        core = lax.bitwise_and(lax.axis_index("subj"), 1)
        even = jnp.where(core == 0, keep, send)
        odd = jnp.where(core == 0, send, keep)
        full = jnp.concatenate(
            [even[:, :quarter], odd[:, :quarter], even[:, quarter:], odd[:, quarter:]], axis=1
        )
        result = lax.psum_scatter(full, "subj", scatter_dimension=1, tiled=True) / subjects
    return field, result


def solution(mesh):
    in_specs = (
        P("subj", "space", None, None),
        P(None, "subj", "space", None, None),
        P(None, "subj", "space", None, None),
        P("space", "subj", None),
        P("subj", "space", None),
        P("subj", "space"),
        P("subj", "space"),
    )
    out_specs = (P(None, "subj", "space", None, None), P("space", "subj", None))
    return jax.shard_map(body, mesh=mesh, in_specs=in_specs, out_specs=out_specs, check_vma=False)
```

```python
import functools

import jax
import jax.numpy as jnp
from jax import lax
from jax.experimental import pallas as pl
from jax.experimental.pallas import tpu as pltpu
from jax.sharding import PartitionSpec as P

BY = 4
RIDGE = 0.25
LANES = 128
LIMIT = 24 * 1024 * 1024
EDGE = 2
CODES = 48
COUNTS = 64
SHIFT = 8

VMEM = pl.BlockSpec(memory_space=pltpu.VMEM)
SMEM = pl.BlockSpec(memory_space=pltpu.SMEM)
ANY = pl.BlockSpec(memory_space=pl.ANY)
SMALL = pl.CostEstimate(flops=0, bytes_accessed=0, transcendentals=0)


def params():
    return pltpu.CompilerParams(vmem_limit_bytes=LIMIT)


def shaped(shape, dtype=jnp.float32):
    return jax.ShapeDtypeStruct(shape, dtype)


def in_hbm(value):
    return pltpu.with_memory_space_constraint(value, pltpu.HBM)


def in_vmem(value):
    return pltpu.with_memory_space_constraint(value, pltpu.VMEM)


def plan_kernel(
    cap,
    counts_in,
    owners_in,
    rows_in,
    images_ref,
    velocity_ref,
    weights_ref,
    request_ref,
    slots_ref,
    held_ref,
    near_ref,
    side_ref,
    counts_ref,
    owners_ref,
    rows_ref,
    v_ref,
    w_ref,
    sems,
):
    subj_dev, rows = rows_ref.shape
    spaces = request_ref.shape[0]
    odd = lax.bitwise_and(lax.axis_index("space"), 1)
    copies = [
        pltpu.make_async_copy(source, target, sems.at[i])
        for i, (source, target) in enumerate(
            (
                (counts_in, counts_ref),
                (owners_in, owners_ref),
                (rows_in, rows_ref),
                (images_ref, held_ref),
                (velocity_ref.at[:, :, pl.ds(0, EDGE)], v_ref.at[1 - odd]),
                (weights_ref.at[:, :, pl.ds(0, EDGE)], w_ref.at[1 - odd]),
                (velocity_ref.at[:, :, pl.ds(rows - EDGE, EDGE)], v_ref.at[odd]),
                (weights_ref.at[:, :, pl.ds(rows - EDGE, EDGE)], w_ref.at[odd]),
            )
        )
    ]
    for copy in copies:
        copy.start()
    for copy in copies[:3]:
        copy.wait()
    t = lax.broadcasted_iota(jnp.int32, (rows, rows), 0)
    u = lax.broadcasted_iota(jnp.int32, (rows, rows), 1)
    eye = t == u
    lane = lax.broadcasted_iota(jnp.int32, (rows, LANES), 1)
    line = lax.broadcasted_iota(jnp.int32, (1, LANES), 1)
    sub = lax.broadcasted_iota(jnp.int32, (spaces, LANES), 0)
    zero = jnp.zeros((rows, rows), jnp.int32)
    request = jnp.zeros((spaces, LANES), jnp.int32)
    extra = jnp.zeros((1, LANES), jnp.int32)
    earlier_subjects = []
    for s in range(subj_dev):
        count = counts_ref[0, s]
        first = lax.shift_right_logical(count, 1)
        owner_u = jnp.broadcast_to(owners_ref[s], (rows, rows))
        row_u = jnp.broadcast_to(rows_ref[s : s + 1, :], (rows, rows))
        owner_t = jnp.broadcast_to(
            jnp.sum(jnp.where(eye, owner_u, zero), axis=1, keepdims=True), (rows, rows)
        )
        row_t = jnp.broadcast_to(
            jnp.sum(jnp.where(eye, row_u, zero), axis=1, keepdims=True), (rows, rows)
        )
        last = rows - (count - first)
        alive_t = (t < first) | (t >= last)
        alive_u = (u < first) | (u >= last)
        same_owner = owner_t == owner_u
        same = same_owner & (row_t == row_u)
        dup_u = jnp.sum(jnp.where(same & alive_t & (t < u), 1, 0), axis=0, keepdims=True)
        dup_t = jnp.sum(jnp.where(same & alive_u & (u < t), 1, 0), axis=1, keepdims=True)
        first_u = alive_u & jnp.broadcast_to(dup_u == 0, (rows, rows))
        first_t = alive_t & jnp.broadcast_to(dup_t == 0, (rows, rows))
        place = jnp.sum(jnp.where(same_owner & first_u & (u < t), 1, 0), axis=1, keepdims=True)
        for owner_v, first_v in earlier_subjects:
            place = place + jnp.sum(
                jnp.where((owner_t == owner_v) & first_v, 1, 0), axis=1, keepdims=True
            )
        earlier_subjects.append((owner_u, first_u))
        slot_t = owner_t * cap + place
        slots_ref[s : s + 1, :] = jnp.sum(
            jnp.where(same & first_t & alive_u, slot_t, zero), axis=0, keepdims=True
        )
        wide_first = jnp.broadcast_to(first_t[:, :1], (rows, LANES))
        wide_owner = jnp.broadcast_to(owner_t[:, :1], (rows, LANES))
        wide_place = jnp.broadcast_to(place, (rows, LANES))
        wide_row = jnp.broadcast_to(row_t[:, :1], (rows, LANES)) + s * rows
        wide_tile = lax.broadcasted_iota(jnp.int32, (rows, LANES), 0)
        hit = jnp.where(wide_first & (wide_place == lane), wide_row, 0)
        for o in range(spaces):
            asked = jnp.sum(jnp.where(wide_owner == o, hit, 0), axis=0, keepdims=True)
            request = request + jnp.where(sub == o, asked, 0)
        counted = jnp.where(wide_first & (wide_owner == lane - COUNTS), 1, 0)
        extra = extra + jnp.sum(counted, axis=0, keepdims=True)
        for side, begin in enumerate((0, rows - EDGE)):
            place = CODES + (side * subj_dev + s) * EDGE
            code = jnp.where(
                wide_tile - begin == lane - place, lax.shift_left(wide_owner, SHIFT) + wide_row, 0
            )
            code = jnp.sum(code, axis=0, keepdims=True)
            extra = extra + jnp.where((line >= place) & (line < place + EDGE), code, 0)
    request_ref[...] = request + jnp.broadcast_to(extra, request.shape)
    for copy in copies[3:]:
        copy.wait()
    for place, out in enumerate((near_ref, side_ref)):
        i = 0
        for c in range(3):
            for s in range(subj_dev):
                for r in range(EDGE):
                    out[i] = v_ref[place, c, s, r].astype(out.dtype)
                    out[i + 1] = w_ref[place, c, s, r]
                    i = i + 2


def plan(counts, owners, local_rows, images, velocity, weights, cap, spaces):
    subj_dev, rows = local_rows.shape
    tile = velocity.shape[3:]
    edge = shaped((2 * EDGE * 3 * subj_dev,) + tile, weights.dtype)
    return pl.pallas_call(
        functools.partial(plan_kernel, cap),
        out_shape=(
            shaped((spaces, LANES), jnp.int32),
            shaped((subj_dev, rows), jnp.int32),
            pltpu.VMEM(images.shape, images.dtype),
            edge,
            edge,
        ),
        in_specs=[ANY] * 6,
        out_specs=(VMEM,) * 5,
        scratch_shapes=[
            pltpu.SMEM(counts.shape, jnp.int32),
            pltpu.VMEM(owners.shape, jnp.int32),
            pltpu.VMEM(local_rows.shape, jnp.int32),
            pltpu.VMEM((2, 3, subj_dev, EDGE) + tile, velocity.dtype),
            pltpu.VMEM((2, 3, subj_dev, EDGE) + tile, weights.dtype),
            pltpu.SemaphoreType.DMA((8,)),
        ],
        compiler_params=params(),
        name="plan",
    )(*map(in_hbm, (counts, owners, local_rows, images, velocity, weights)))


def edge_codes(wanted_ref, me, subj_dev):
    spaces = wanted_ref.shape[0]
    before, after = jnp.maximum(me - 1, 0), jnp.minimum(me + 1, spaces - 1)
    found = []
    for i in range(subj_dev * EDGE):
        found.append((wanted_ref[before, CODES + subj_dev * EDGE + i], me > 0))
    for i in range(subj_dev * EDGE):
        found.append((wanted_ref[after, CODES + i], me < spaces - 1))
    return found


def crowded(wanted, base, size, subj_dev):
    spaces, lanes = wanted.shape
    d = lax.broadcasted_iota(jnp.int32, (spaces, lanes), 0)
    owner = lax.broadcasted_iota(jnp.int32, (spaces, lanes), 1) - COUNTS
    need = wanted
    for side in range(2):
        codes = pltpu.roll(wanted, 1 if side == 0 else spaces - 1, 0)
        valid = d > 0 if side == 0 else d < spaces - 1
        begin = CODES + (subj_dev * EDGE if side == 0 else 0)
        for i in range(subj_dev * EDGE):
            code = jnp.broadcast_to(codes[:, begin + i : begin + i + 1], (spaces, lanes))
            hit = valid & (lax.shift_right_logical(code, SHIFT) == owner)
            need = need + jnp.where(hit, 1, 0)
    pair = (owner >= 0) & (owner < spaces) & (lax.bitwise_xor(owner, d) >= base)
    over = jnp.where(pair & (need > size), 1.0, 0.0)
    return jnp.max(jnp.max(over, axis=0, keepdims=True), axis=1, keepdims=True)


def whole_row(shares, r, position):
    parts = [share[r] for share in shares]
    mask = 1
    while mask < len(shares):
        turned = lax.bitwise_and(position, mask) > 0
        parts = [jnp.where(turned, parts[i ^ mask], part) for i, part in enumerate(parts)]
        mask = 2 * mask
    return jnp.concatenate(parts, axis=0)


def carries(spaces):
    return [k for k in range(3, spaces) if k & (k + 1) == 0]


def pick_kernel(cap, base, total, groups, wanted_ref, requests_ref, images_ref, near_ref, *refs):
    shares, refs = refs[:groups], refs[groups + 1 :]
    spaces = requests_ref.shape[0]
    sends, overs = refs[:spaces], refs[spaces : 2 * spaces - base]
    edge_slots, over_ref, used = refs[-3:]
    rows = shares[0].shape[0]
    subj_dev = (total - cap) // (2 * EDGE)
    me, position = lax.axis_index("space"), lax.axis_index("subj")
    odd = lax.bitwise_and(me, 1)
    short = sends[-1].shape[0] - 2 * EDGE
    for k in range(spaces):
        target = lax.bitwise_xor(me, k)
        size = short if k >= base else total

        def put(c, brick, k=k, size=size):
            if isinstance(c, int):
                ref, c = (sends[k], c) if c < size else (overs[k - base], c - size)
                ref[c] = brick
            elif k < base:
                sends[k][c] = brick
            else:

                @pl.when(c < size)
                def _():
                    sends[k][c] = brick

                @pl.when(c >= size)
                def _():
                    overs[k - base][c - size] = brick

        for c in range(cap):
            put(c, images_ref[wanted_ref[target, c]])
        place = wanted_ref[target, COUNTS + me]
        for code, valid in edge_codes(wanted_ref, target, subj_dev):
            mine = valid & (lax.shift_right_logical(code, SHIFT) == me)

            @pl.when(mine)
            def _(code=code, place=place, put=put):
                put(place, images_ref[lax.bitwise_and(code, (1 << SHIFT) - 1)])

            place = place + jnp.where(mine, 1, 0)
    over_ref[0] = jnp.max(crowded(requests_ref[...], base, short, subj_dev)).astype(jnp.int32)
    for o in range(spaces):
        used[o] = wanted_ref[me, COUNTS + o]
    for i, (code, valid) in enumerate(edge_codes(wanted_ref, me, subj_dev)):
        owner = jnp.where(valid, lax.shift_right_logical(code, SHIFT), 0)
        place = used[owner]
        edge_slots[i] = jnp.where(valid, lax.bitwise_xor(owner, me) * total + place, 0)
        used[owner] = place + jnp.where(valid, 1, 0)
    for i in range(near_ref.shape[0]):
        sends[1][total + 2 * EDGE + i] = near_ref[i]
    for r in range(EDGE):
        low = whole_row(shares, r, position)
        high = whole_row(shares, rows - EDGE + r, position)
        for k in [1, *carries(spaces)]:
            value = jnp.where((odd == 1) == (k == 1), low, high)
            at = (short if k >= base else total) + 2 * r
            rounded = value.astype(sends[k].dtype)
            sends[k][at] = rounded
            sends[k][at + 1] = (value - rounded.astype(jnp.float32)).astype(sends[k].dtype)


def pick(wanted, images, near, shares, side, cap, sizes):
    spaces = wanted.shape[0]
    base = sizes.index(min(sizes))
    total = sizes[0]
    tile = images.shape[1:]
    longer = [n + 2 * EDGE * (k == 1 or k in carries(spaces)) for k, n in enumerate(sizes)]
    longer[1] += near.shape[0]
    outs = [shaped((n,) + tile, images.dtype) for n in longer]
    outs += [shaped((total - n,) + tile, images.dtype) for n in sizes[base:]]
    edges = total - cap
    got = pl.pallas_call(
        functools.partial(pick_kernel, cap, base, total, len(shares)),
        out_shape=outs + [shaped((edges,), jnp.int32), shaped((1,), jnp.int32)],
        in_specs=[SMEM] + [VMEM] * (3 + len(shares)) + [ANY],
        out_specs=[VMEM] * len(outs) + [SMEM, SMEM],
        scratch_shapes=[pltpu.SMEM((spaces,), jnp.int32)],
        compiler_params=params(),
        name="pick",
    )(wanted, wanted, images, near, *shares, side)
    return got[:spaces], got[spaces:-2], *got[-2:]


def up_x(v):
    return pltpu.roll(v, v.shape[0] - BY, 0)


def up_y(v):
    return pltpu.roll(v, v.shape[0] - 1, 0)


def up_z(v):
    return pltpu.roll(v, v.shape[1] - 1, 1)


def down_x(v):
    return pltpu.roll(v, BY, 0)


def down_y(v):
    return pltpu.roll(v, 1, 0)


def down_z(v):
    return pltpu.roll(v, 1, 1)


def inside(shape, value):
    p = lax.broadcasted_iota(jnp.int32, shape, 0)
    z = lax.broadcasted_iota(jnp.int32, shape, 1)
    y = lax.bitwise_and(p, BY - 1)
    conditions = (
        p < shape[0] - BY,
        p >= BY,
        y < BY - 1,
        y > 0,
        z < shape[1] - 1,
        z > 0,
    )
    return [jnp.where(c, value, 0.0).astype(jnp.float32) for c in conditions]


def warp_tile(brick, fractions, masks, live):
    frac_x, frac_y, frac_z = (f.astype(jnp.float32) for f in fractions)
    high_x, high_y, high_z = frac_x * masks[0], frac_y * masks[2], frac_z * masks[4]
    low_x, low_y, low_z = 1.0 - frac_x, 1.0 - frac_y, 1.0 - frac_z
    low_x, high_x = low_x * live, high_x * live

    def along_z(v):
        return low_z * v + high_z * up_z(v)

    def along_y(v):
        return low_y * along_z(v) + high_y * along_z(up_y(v))

    return low_x * along_y(brick) + high_x * along_y(up_x(brick))


def slopes(w, halves):
    return (
        up_x(w) * halves[0] - down_x(w) * halves[1],
        up_y(w) * halves[2] - down_y(w) * halves[3],
        up_z(w) * halves[4] - down_z(w) * halves[5],
    )


def predict(w, g, f):
    return w + (g[0] * f[0] + g[1] * f[1]) + g[2] * f[2]


def smooth(before, here, after, masks):
    rowwise = (before + after) + (here + here)
    return (down_z(rowwise) * masks[5] + up_z(rowwise) * masks[4]) + (rowwise + rowwise)


def first_kernel(spaces, base, groups, *refs):
    counts_ref, slots_ref, edge_slots_ref = refs[:3]
    parts, refs = refs[3 : 3 + spaces], refs[3 + spaces :]
    overs, refs = refs[: spaces - base], refs[spaces - base :]
    shares, refs = refs[:groups], refs[groups:]
    side_ref, weights_in, velocity_in = refs[:3]
    warped_ref, slopes_ref, scale_ref, field_ref, keep_ref, send_ref = refs[3:9]
    table, update, weights_ref, packs, chunk_sems = refs[9:]
    _, subj_dev, rows, plane, depth = weights_ref.shape
    total = parts[0].shape[0]
    short = parts[-1].shape[0] - 2 * EDGE
    cap = total - 2 * EDGE * subj_dev
    me, position = lax.axis_index("space"), lax.axis_index("subj")
    core = lax.bitwise_and(position, 1)
    odd = lax.bitwise_and(me, 1)
    chunks = chunk_sems.shape[0] // 2
    chunk = rows // chunks
    chunk_copies = []
    for i in range(chunks):
        part = pl.ds(i * chunk, chunk)
        chunk_copies.append(
            [
                pltpu.make_async_copy(source.at[:, :, part], target, chunk_sems.at[n])
                for n, source, target in (
                    (2 * i, weights_in, weights_ref.at[:, :, part]),
                    (2 * i + 1, velocity_in, field_ref.at[:, :, pl.ds(1 + i * chunk, chunk)]),
                )
            ]
        )
    for copy in sum(chunk_copies, []):
        copy.start()
    for k in range(spaces):
        for c in range(total):
            if k < base or c < short:
                table[k * total + c] = parts[k][c]
            else:
                table[k * total + c] = overs[k - base][c - short]
    for i in range(side_ref.shape[0]):
        packs[1 - odd, 2 * EDGE + i] = parts[1][total + 2 * EDGE + i]
        packs[odd, 2 * EDGE + i] = side_ref[i]
    for i in range(2 * EDGE):
        packs[1 - odd, i] = parts[1][total + i]
        packs[odd, i] = jnp.zeros_like(side_ref[0])
    other = lax.bitwise_xor(me, me - 1 + 2 * odd)
    for k in carries(spaces):

        @pl.when(other == k)
        def _(k=k):
            for i in range(2 * EDGE):
                packs[odd, i] = parts[k][(short if k >= base else total) + i]

    before_ref, after_ref = packs.at[0], packs.at[1]
    masks, halves = inside((plane, depth), 1.0), inside((plane, depth), 0.5)

    def tile(s, e, brick, fractions, live, f, current):
        w = warp_tile(brick.astype(jnp.float32), fractions, masks, live)
        g = slopes(w, halves)
        scale = 0.0625 / (g[0] * g[0] + g[1] * g[1] + g[2] * g[2] + RIDGE)
        ratio = (predict(w, g, f) - current) * scale
        warped_ref[s, e] = w
        scale_ref[s, e] = scale
        for c in range(3):
            slopes_ref[c, s, e] = g[c]
            update[c, s, e] = g[c] * ratio

    def row(r, carry):
        current = whole_row(shares, r, position)
        for s in range(subj_dev):
            count = counts_ref[0, s]
            first = lax.shift_right_logical(count, 1)
            alive = (r < first) | (r >= rows - (count - first))
            live = jnp.where(alive, 1.0, 0.0).astype(jnp.float32)
            wanted = slots_ref[s, r]
            owner = lax.div(wanted, cap)
            slot = lax.bitwise_xor(owner, me) * total + (wanted - owner * cap)
            tile(
                s,
                r + EDGE,
                table[slot],
                [weights_ref[c, s, r] for c in range(3)],
                live,
                [field_ref[c, s, r + 1] for c in range(3)],
                current,
            )
        return carry

    for side, (ref, there, e0) in enumerate(
        ((before_ref, me > 0, 0), (after_ref, me < spaces - 1, rows + EDGE))
    ):
        live = jnp.where(there, 1.0, 0.0).astype(jnp.float32)
        for r in range(EDGE):
            current = ref[2 * r].astype(jnp.float32) + ref[2 * r + 1].astype(jnp.float32)
            for s in range(subj_dev):
                at = [2 * ((c * subj_dev + s + 1) * EDGE + r) for c in range(3)]
                tile(
                    s,
                    e0 + r,
                    table[edge_slots_ref[(side * subj_dev + s) * EDGE + r]],
                    [ref[a + 1] for a in at],
                    live,
                    [ref[a].astype(jnp.float32) for a in at],
                    current,
                )

    for i in range(chunks):
        for copy in chunk_copies[i]:
            copy.wait()
        lax.fori_loop(i * chunk, (i + 1) * chunk, row, 0, unroll=8)

    for c in range(3):
        for s in range(subj_dev):
            at = 2 * (c * subj_dev + s + 1) * EDGE
            field_ref[c, s, 0] = before_ref[at + 2 * (EDGE - 1)].astype(jnp.float32)
            field_ref[c, s, rows + 1] = after_ref[at].astype(jnp.float32)

    def move(i, carry):
        e = i + EDGE - 1
        total_p = None
        for s in range(subj_dev):
            g = [slopes_ref[c, s, e] for c in range(3)]
            f = []
            for c in range(3):
                delta = smooth(update[c, s, e - 1], update[c, s, e], update[c, s, e + 1], masks)
                f.append(field_ref[c, s, i] - delta)
                field_ref[c, s, i] = f[c]
            p = predict(warped_ref[s, e], g, f)
            total_p = p if total_p is None else total_p + p
        half = plane // 2
        low, high = total_p[:half], total_p[half:]
        keep_ref[i] = jnp.where(core == 0, low, high)
        send_ref[i] = jnp.where(core == 0, high, low)
        return carry

    lax.fori_loop(0, rows + 2, move, 0, unroll=22)


def first(counts, slots, edge_slots, parts, overs, shares, side, weights, velocity):
    _, subj_dev, rows, plane, depth = velocity.shape
    spaces = len(parts)
    total = parts[0].shape[0]
    long = rows + 2 * EDGE
    sums = shaped((rows + 2, plane // 2, depth))
    arrays = [*parts, *overs, *shares, side]
    return pl.pallas_call(
        functools.partial(first_kernel, spaces, spaces - len(overs), len(shares)),
        out_shape=(
            shaped((subj_dev, long, plane, depth)),
            shaped((3, subj_dev, long, plane, depth)),
            shaped((subj_dev, long, plane, depth)),
            shaped((3, subj_dev, rows + 2, plane, depth)),
            sums,
            sums,
        ),
        in_specs=[SMEM] * 3 + [VMEM] * len(arrays) + [ANY] * 2,
        out_specs=(VMEM,) * 6,
        scratch_shapes=[
            pltpu.VMEM((spaces * total, plane, depth), weights.dtype),
            pltpu.VMEM((3, subj_dev, long, plane, depth), jnp.float32),
            pltpu.VMEM(weights.shape, weights.dtype),
            pltpu.VMEM((2, side.shape[0] + 2 * EDGE) + side.shape[1:], side.dtype),
            pltpu.SemaphoreType.DMA((16,)),
        ],
        compiler_params=params(),
        name="first",
    )(counts, slots, edge_slots, *arrays, in_hbm(weights), in_hbm(velocity))


def last_kernel(
    mine_ref,
    other_ref,
    warped_ref,
    slopes_ref,
    scale_ref,
    field_ref,
    out_ref,
    keep_ref,
    send_ref,
    update,
    out,
    sems,
):
    _, subj_dev, rows, plane, depth = out.shape
    core = lax.bitwise_and(lax.axis_index("subj"), 1)
    masks = inside((plane, depth), 1.0)
    chunks = sems.shape[0]
    chunk = rows // chunks

    def renew(i, carry):
        mine, other = mine_ref[i].astype(jnp.float32), other_ref[i].astype(jnp.float32)
        current = jnp.concatenate(
            [jnp.where(core == 0, mine, other), jnp.where(core == 0, other, mine)], axis=0
        )
        for s in range(subj_dev):
            g = [slopes_ref[c, s, i + 1] for c in range(3)]
            f = [field_ref[c, s, i] for c in range(3)]
            ratio = (predict(warped_ref[s, i + 1], g, f) - current) * scale_ref[s, i + 1]
            for c in range(3):
                update[c, s, i] = g[c] * ratio
        return carry

    lax.fori_loop(0, rows + 2, renew, 0, unroll=22)

    def move(r, carry):
        total = None
        for s in range(subj_dev):
            g = [slopes_ref[c, s, r + EDGE] for c in range(3)]
            f = []
            for c in range(3):
                delta = smooth(update[c, s, r], update[c, s, r + 1], update[c, s, r + 2], masks)
                f.append(field_ref[c, s, r + 1] - delta)
                out[c, s, r] = f[c]
            p = predict(warped_ref[s, r + EDGE], g, f)
            total = p if total is None else total + p
        quarter = plane // 4
        low, high = total[: 2 * quarter], total[2 * quarter :]
        upper = lax.broadcasted_iota(jnp.int32, low.shape, 0) >= quarter
        even = jnp.where(upper, pltpu.roll(high, quarter, 0), low)
        odd = jnp.where(upper, high, pltpu.roll(low, quarter, 0))
        keep_ref[r] = jnp.where(core == 0, even, odd)
        send_ref[r] = jnp.where(core == 0, odd, even)
        return carry

    copies = []
    for i in range(chunks):
        lax.fori_loop(i * chunk, (i + 1) * chunk, move, 0, unroll=8)
        part = pl.ds(i * chunk, chunk)
        copy = pltpu.make_async_copy(out.at[:, :, part], out_ref.at[:, :, part], sems.at[i])
        copy.start()
        copies.append(copy)
    for copy in copies:
        copy.wait()


def last(mine, other, warped, slopes_all, scale, field, rows):
    _, subj_dev, _, plane, depth = field.shape
    shape = (3, subj_dev, rows, plane, depth)
    sums = shaped((rows, plane // 2, depth))
    return pl.pallas_call(
        last_kernel,
        out_shape=(shaped(shape), sums, sums),
        in_specs=[VMEM] * 6,
        out_specs=(ANY, VMEM, VMEM),
        scratch_shapes=[
            pltpu.VMEM(field.shape, jnp.float32),
            pltpu.VMEM(shape, jnp.float32),
            pltpu.SemaphoreType.DMA((8,)),
        ],
        compiler_params=params(),
        name="last",
    )(mine, other, warped, slopes_all, scale, field)


def fold_kernel(keep_ref, got_ref, own_ref, away_ref):
    second = lax.shift_right_logical(lax.axis_index("subj"), 1) == 1
    quarter = own_ref.shape[1]

    def row(r, carry):
        total = keep_ref[r] + got_ref[r]
        low, high = total[:quarter], total[quarter:]
        own_ref[r] = jnp.where(second, high, low)
        away_ref[r] = jnp.where(second, low, high)
        return carry

    lax.fori_loop(0, keep_ref.shape[0], row, 0, unroll=8)


def fold(keep, got):
    rows, half, depth = keep.shape
    part = shaped((rows, half // 2, depth))
    return pl.pallas_call(
        fold_kernel,
        out_shape=(part, part),
        in_specs=[VMEM] * 2,
        out_specs=(VMEM,) * 2,
        compiler_params=params(),
        name="fold",
    )(keep, got)


def swap(value, axis, mask):
    count = lax.axis_size(axis)
    return lax.ppermute(value, axis, [(i, i ^ mask) for i in range(count)])


def body(images, velocity, weights, template, owners, local_rows, tile_counts):
    spaces = lax.axis_size("space")
    groups = lax.axis_size("subj")
    subj_dev, rows, plane, depth = images.shape
    cap = subj_dev * (2 * rows // spaces)
    subjects = subj_dev * groups
    counts = jnp.swapaxes(tile_counts, 0, 1)

    request, slots, held, near_pack, side = plan(
        counts,
        jnp.swapaxes(owners, 1, 2),
        local_rows,
        images.reshape(subj_dev * rows, plane, depth),
        velocity,
        weights,
        cap,
        spaces,
    )
    others = [(i, i + 1) for i in range(1, spaces - 1, 2)]
    side = lax.ppermute(side, "space", others + [(j, i) for i, j in others])
    shares = [template] + [swap(template, "subj", k) for k in range(1, groups)]
    wanted = lax.all_to_all(request, "space", split_axis=0, concat_axis=0, tiled=True)

    base = spaces // 2
    total = cap + 2 * EDGE * subj_dev
    short = cap - cap // 8
    sizes = [total] * base + [short] * (spaces - base)
    sends, overs, edge_slots, over = pick(wanted, held, near_pack, shares, side, cap, sizes)
    far = [swap(sends[k], "space", k) for k in range(base, spaces)]
    near = [sends[0]] + [swap(sends[k], "space", k) for k in range(1, base)]

    def again(state):
        parts = [swap(part, "space", base + i) for i, part in enumerate(state[1])]
        return jnp.int32(0), parts

    _, overs = lax.while_loop(lambda state: state[0] > 0, again, (over[0], list(overs)))

    warped, slopes_all, scale, field, keep, send = first(
        counts, slots, edge_slots, near + far, overs, shares, side, weights, velocity
    )
    share = keep + swap(send, "subj", 1)
    mask = 2
    while mask < groups:
        share = share + swap(share.astype(jnp.bfloat16), "subj", mask).astype(jnp.float32)
        mask = 2 * mask
    mine = (share / subjects).astype(jnp.bfloat16)
    other = swap(mine, "subj", 1)

    field, keep, send = last(mine, other, warped, slopes_all, scale, field, rows)
    if groups == 4:
        own, away = fold(keep, swap(send, "subj", 1))
        result = (own + swap(away, "subj", 2)) / subjects
    else:
        quarter = plane // 4
        core = lax.bitwise_and(lax.axis_index("subj"), 1)
        even = jnp.where(core == 0, keep, send)
        odd = jnp.where(core == 0, send, keep)
        full = jnp.concatenate(
            [even[:, :quarter], odd[:, :quarter], even[:, quarter:], odd[:, quarter:]], axis=1
        )
        result = lax.psum_scatter(full, "subj", scatter_dimension=1, tiled=True) / subjects
    return field, result


def solution(mesh):
    in_specs = (
        P("subj", "space", None, None),
        P(None, "subj", "space", None, None),
        P(None, "subj", "space", None, None),
        P("space", "subj", None),
        P("subj", "space", None),
        P("subj", "space"),
        P("subj", "space"),
    )
    out_specs = (P(None, "subj", "space", None, None), P("space", "subj", None))
    return jax.shard_map(body, mesh=mesh, in_specs=in_specs, out_specs=out_specs, check_vma=False)
```

```python
import functools

import jax
import jax.numpy as jnp
from jax import lax
from jax.experimental import pallas as pl
from jax.experimental.pallas import tpu as pltpu
from jax.sharding import PartitionSpec as P

BY = 4
RIDGE = 0.25
LANES = 128
LIMIT = 24 * 1024 * 1024
EDGE = 2
CODES = 48
COUNTS = 64
SHIFT = 8

VMEM = pl.BlockSpec(memory_space=pltpu.VMEM)
SMEM = pl.BlockSpec(memory_space=pltpu.SMEM)
ANY = pl.BlockSpec(memory_space=pl.ANY)
SMALL = pl.CostEstimate(flops=0, bytes_accessed=0, transcendentals=0)


def params():
    return pltpu.CompilerParams(vmem_limit_bytes=LIMIT)


def shaped(shape, dtype=jnp.float32):
    return jax.ShapeDtypeStruct(shape, dtype)


def in_hbm(value):
    return pltpu.with_memory_space_constraint(value, pltpu.HBM)


def in_vmem(value):
    return pltpu.with_memory_space_constraint(value, pltpu.VMEM)


def plan_kernel(
    cap,
    counts_in,
    owners_in,
    rows_in,
    images_ref,
    velocity_ref,
    weights_ref,
    request_ref,
    slots_ref,
    held_ref,
    near_ref,
    side_ref,
    counts_ref,
    owners_ref,
    rows_ref,
    v_ref,
    w_ref,
    sems,
):
    subj_dev, rows = rows_ref.shape
    spaces = request_ref.shape[0]
    odd = lax.bitwise_and(lax.axis_index("space"), 1)
    copies = [
        pltpu.make_async_copy(source, target, sems.at[i])
        for i, (source, target) in enumerate(
            (
                (counts_in, counts_ref),
                (owners_in, owners_ref),
                (rows_in, rows_ref),
                (images_ref, held_ref),
                (velocity_ref.at[:, :, pl.ds(0, EDGE)], v_ref.at[1 - odd]),
                (weights_ref.at[:, :, pl.ds(0, EDGE)], w_ref.at[1 - odd]),
                (velocity_ref.at[:, :, pl.ds(rows - EDGE, EDGE)], v_ref.at[odd]),
                (weights_ref.at[:, :, pl.ds(rows - EDGE, EDGE)], w_ref.at[odd]),
            )
        )
    ]
    for copy in copies:
        copy.start()
    for copy in copies[:3]:
        copy.wait()
    t = lax.broadcasted_iota(jnp.int32, (rows, rows), 0)
    u = lax.broadcasted_iota(jnp.int32, (rows, rows), 1)
    eye = t == u
    lane = lax.broadcasted_iota(jnp.int32, (rows, LANES), 1)
    line = lax.broadcasted_iota(jnp.int32, (1, LANES), 1)
    sub = lax.broadcasted_iota(jnp.int32, (spaces, LANES), 0)
    zero = jnp.zeros((rows, rows), jnp.int32)
    request = jnp.zeros((spaces, LANES), jnp.int32)
    extra = jnp.zeros((1, LANES), jnp.int32)
    earlier_subjects = []
    for s in range(subj_dev):
        count = counts_ref[0, s]
        first = lax.shift_right_logical(count, 1)
        owner_u = jnp.broadcast_to(owners_ref[s], (rows, rows))
        row_u = jnp.broadcast_to(rows_ref[s : s + 1, :], (rows, rows))
        owner_t = jnp.broadcast_to(
            jnp.sum(jnp.where(eye, owner_u, zero), axis=1, keepdims=True), (rows, rows)
        )
        row_t = jnp.broadcast_to(
            jnp.sum(jnp.where(eye, row_u, zero), axis=1, keepdims=True), (rows, rows)
        )
        last = rows - (count - first)
        alive_t = (t < first) | (t >= last)
        alive_u = (u < first) | (u >= last)
        same_owner = owner_t == owner_u
        same = same_owner & (row_t == row_u)
        dup_u = jnp.sum(jnp.where(same & alive_t & (t < u), 1, 0), axis=0, keepdims=True)
        dup_t = jnp.sum(jnp.where(same & alive_u & (u < t), 1, 0), axis=1, keepdims=True)
        first_u = alive_u & jnp.broadcast_to(dup_u == 0, (rows, rows))
        first_t = alive_t & jnp.broadcast_to(dup_t == 0, (rows, rows))
        place = jnp.sum(jnp.where(same_owner & first_u & (u < t), 1, 0), axis=1, keepdims=True)
        for owner_v, first_v in earlier_subjects:
            place = place + jnp.sum(
                jnp.where((owner_t == owner_v) & first_v, 1, 0), axis=1, keepdims=True
            )
        earlier_subjects.append((owner_u, first_u))
        slot_t = owner_t * cap + place
        slots_ref[s : s + 1, :] = jnp.sum(
            jnp.where(same & first_t & alive_u, slot_t, zero), axis=0, keepdims=True
        )
        wide_first = jnp.broadcast_to(first_t[:, :1], (rows, LANES))
        wide_owner = jnp.broadcast_to(owner_t[:, :1], (rows, LANES))
        wide_place = jnp.broadcast_to(place, (rows, LANES))
        wide_row = jnp.broadcast_to(row_t[:, :1], (rows, LANES)) + s * rows
        wide_tile = lax.broadcasted_iota(jnp.int32, (rows, LANES), 0)
        hit = jnp.where(wide_first & (wide_place == lane), wide_row, 0)
        for o in range(spaces):
            asked = jnp.sum(jnp.where(wide_owner == o, hit, 0), axis=0, keepdims=True)
            request = request + jnp.where(sub == o, asked, 0)
        counted = jnp.where(wide_first & (wide_owner == lane - COUNTS), 1, 0)
        extra = extra + jnp.sum(counted, axis=0, keepdims=True)
        for side, begin in enumerate((0, rows - EDGE)):
            place = CODES + (side * subj_dev + s) * EDGE
            code = jnp.where(
                wide_tile - begin == lane - place, lax.shift_left(wide_owner, SHIFT) + wide_row, 0
            )
            code = jnp.sum(code, axis=0, keepdims=True)
            extra = extra + jnp.where((line >= place) & (line < place + EDGE), code, 0)
    request_ref[...] = request + jnp.broadcast_to(extra, request.shape)
    for copy in copies[3:]:
        copy.wait()
    for place, out in enumerate((near_ref, side_ref)):
        i = 0
        for c in range(3):
            for s in range(subj_dev):
                for r in range(EDGE):
                    out[i] = v_ref[place, c, s, r].astype(out.dtype)
                    out[i + 1] = w_ref[place, c, s, r]
                    i = i + 2


def plan(counts, owners, local_rows, images, velocity, weights, cap, spaces):
    subj_dev, rows = local_rows.shape
    tile = velocity.shape[3:]
    edge = shaped((2 * EDGE * 3 * subj_dev,) + tile, weights.dtype)
    return pl.pallas_call(
        functools.partial(plan_kernel, cap),
        out_shape=(
            shaped((spaces, LANES), jnp.int32),
            shaped((subj_dev, rows), jnp.int32),
            pltpu.VMEM(images.shape, images.dtype),
            edge,
            edge,
        ),
        in_specs=[ANY] * 6,
        out_specs=(VMEM,) * 5,
        scratch_shapes=[
            pltpu.SMEM(counts.shape, jnp.int32),
            pltpu.VMEM(owners.shape, jnp.int32),
            pltpu.VMEM(local_rows.shape, jnp.int32),
            pltpu.VMEM((2, 3, subj_dev, EDGE) + tile, velocity.dtype),
            pltpu.VMEM((2, 3, subj_dev, EDGE) + tile, weights.dtype),
            pltpu.SemaphoreType.DMA((8,)),
        ],
        compiler_params=params(),
        name="plan",
    )(*map(in_hbm, (counts, owners, local_rows, images, velocity, weights)))


def edge_codes(wanted_ref, me, subj_dev):
    spaces = wanted_ref.shape[0]
    before, after = jnp.maximum(me - 1, 0), jnp.minimum(me + 1, spaces - 1)
    found = []
    for i in range(subj_dev * EDGE):
        found.append((wanted_ref[before, CODES + subj_dev * EDGE + i], me > 0))
    for i in range(subj_dev * EDGE):
        found.append((wanted_ref[after, CODES + i], me < spaces - 1))
    return found


def crowded(wanted, base, size, subj_dev):
    spaces, lanes = wanted.shape
    d = lax.broadcasted_iota(jnp.int32, (spaces, lanes), 0)
    owner = lax.broadcasted_iota(jnp.int32, (spaces, lanes), 1) - COUNTS
    need = wanted
    for side in range(2):
        codes = pltpu.roll(wanted, 1 if side == 0 else spaces - 1, 0)
        valid = d > 0 if side == 0 else d < spaces - 1
        begin = CODES + (subj_dev * EDGE if side == 0 else 0)
        for i in range(subj_dev * EDGE):
            code = jnp.broadcast_to(codes[:, begin + i : begin + i + 1], (spaces, lanes))
            hit = valid & (lax.shift_right_logical(code, SHIFT) == owner)
            need = need + jnp.where(hit, 1, 0)
    pair = (owner >= 0) & (owner < spaces) & (lax.bitwise_xor(owner, d) >= base)
    over = jnp.where(pair & (need > size), 1.0, 0.0)
    return jnp.max(jnp.max(over, axis=0, keepdims=True), axis=1, keepdims=True)


def whole_row(shares, r, position):
    parts = [share[r] for share in shares]
    mask = 1
    while mask < len(shares):
        turned = lax.bitwise_and(position, mask) > 0
        parts = [jnp.where(turned, parts[i ^ mask], part) for i, part in enumerate(parts)]
        mask = 2 * mask
    return jnp.concatenate(parts, axis=0)


def carries(spaces):
    return [k for k in range(3, spaces) if k & (k + 1) == 0]


def pick_kernel(cap, base, total, groups, wanted_ref, requests_ref, images_ref, near_ref, *refs):
    shares, refs = refs[:groups], refs[groups + 1 :]
    spaces = requests_ref.shape[0]
    sends, overs = refs[:spaces], refs[spaces : 2 * spaces - base]
    edge_slots, over_ref, used = refs[-3:]
    rows = shares[0].shape[0]
    subj_dev = (total - cap) // (2 * EDGE)
    me, position = lax.axis_index("space"), lax.axis_index("subj")
    odd = lax.bitwise_and(me, 1)
    short = sends[-1].shape[0] - 2 * EDGE
    for k in range(spaces):
        target = lax.bitwise_xor(me, k)
        size = short if k >= base else total

        def put(c, brick, k=k, size=size):
            if isinstance(c, int):
                ref, c = (sends[k], c) if c < size else (overs[k - base], c - size)
                ref[c] = brick
            elif k < base:
                sends[k][c] = brick
            else:

                @pl.when(c < size)
                def _():
                    sends[k][c] = brick

                @pl.when(c >= size)
                def _():
                    overs[k - base][c - size] = brick

        for c in range(cap):
            put(c, images_ref[wanted_ref[target, c]])
        place = wanted_ref[target, COUNTS + me]
        for code, valid in edge_codes(wanted_ref, target, subj_dev):
            mine = valid & (lax.shift_right_logical(code, SHIFT) == me)

            @pl.when(mine)
            def _(code=code, place=place, put=put):
                put(place, images_ref[lax.bitwise_and(code, (1 << SHIFT) - 1)])

            place = place + jnp.where(mine, 1, 0)
    over_ref[0] = jnp.max(crowded(requests_ref[...], base, short, subj_dev)).astype(jnp.int32)
    for o in range(spaces):
        used[o] = wanted_ref[me, COUNTS + o]
    for i, (code, valid) in enumerate(edge_codes(wanted_ref, me, subj_dev)):
        owner = jnp.where(valid, lax.shift_right_logical(code, SHIFT), 0)
        place = used[owner]
        edge_slots[i] = jnp.where(valid, lax.bitwise_xor(owner, me) * total + place, 0)
        used[owner] = place + jnp.where(valid, 1, 0)
    for i in range(near_ref.shape[0]):
        sends[1][total + 2 * EDGE + i] = near_ref[i]
    for r in range(EDGE):
        low = whole_row(shares, r, position)
        high = whole_row(shares, rows - EDGE + r, position)
        for k in [1, *carries(spaces)]:
            value = jnp.where((odd == 1) == (k == 1), low, high)
            at = (short if k >= base else total) + 2 * r
            rounded = value.astype(sends[k].dtype)
            sends[k][at] = rounded
            sends[k][at + 1] = (value - rounded.astype(jnp.float32)).astype(sends[k].dtype)


def pick(wanted, images, near, shares, side, cap, sizes):
    spaces = wanted.shape[0]
    base = sizes.index(min(sizes))
    total = sizes[0]
    tile = images.shape[1:]
    longer = [n + 2 * EDGE * (k == 1 or k in carries(spaces)) for k, n in enumerate(sizes)]
    longer[1] += near.shape[0]
    outs = [shaped((n,) + tile, images.dtype) for n in longer]
    outs += [shaped((total - n,) + tile, images.dtype) for n in sizes[base:]]
    edges = total - cap
    got = pl.pallas_call(
        functools.partial(pick_kernel, cap, base, total, len(shares)),
        out_shape=outs + [shaped((edges,), jnp.int32), shaped((1,), jnp.int32)],
        in_specs=[SMEM] + [VMEM] * (3 + len(shares)) + [ANY],
        out_specs=[VMEM] * len(outs) + [SMEM, SMEM],
        scratch_shapes=[pltpu.SMEM((spaces,), jnp.int32)],
        compiler_params=params(),
        name="pick",
    )(wanted, wanted, images, near, *shares, side)
    return got[:spaces], got[spaces:-2], *got[-2:]


def up_x(v):
    return pltpu.roll(v, v.shape[0] - BY, 0)


def up_y(v):
    return pltpu.roll(v, v.shape[0] - 1, 0)


def up_z(v):
    return pltpu.roll(v, v.shape[1] - 1, 1)


def down_x(v):
    return pltpu.roll(v, BY, 0)


def down_y(v):
    return pltpu.roll(v, 1, 0)


def down_z(v):
    return pltpu.roll(v, 1, 1)


def inside(shape, value):
    p = lax.broadcasted_iota(jnp.int32, shape, 0)
    z = lax.broadcasted_iota(jnp.int32, shape, 1)
    y = lax.bitwise_and(p, BY - 1)
    conditions = (
        p < shape[0] - BY,
        p >= BY,
        y < BY - 1,
        y > 0,
        z < shape[1] - 1,
        z > 0,
    )
    return [jnp.where(c, value, 0.0).astype(jnp.float32) for c in conditions]


def warp_tile(brick, fractions, masks, live):
    frac_x, frac_y, frac_z = (f.astype(jnp.float32) for f in fractions)
    high_x, high_y, high_z = frac_x * masks[0], frac_y * masks[2], frac_z * masks[4]
    low_x, low_y, low_z = 1.0 - frac_x, 1.0 - frac_y, 1.0 - frac_z
    low_x, high_x = low_x * live, high_x * live

    def along_z(v):
        return low_z * v + high_z * up_z(v)

    def along_y(v):
        return low_y * along_z(v) + high_y * along_z(up_y(v))

    return low_x * along_y(brick) + high_x * along_y(up_x(brick))


def slopes(w, halves):
    return (
        up_x(w) * halves[0] - down_x(w) * halves[1],
        up_y(w) * halves[2] - down_y(w) * halves[3],
        up_z(w) * halves[4] - down_z(w) * halves[5],
    )


def predict(w, g, f):
    return w + (g[0] * f[0] + g[1] * f[1]) + g[2] * f[2]


def smooth(before, here, after, masks):
    rowwise = (before + after) + (here + here)
    return (down_z(rowwise) * masks[5] + up_z(rowwise) * masks[4]) + (rowwise + rowwise)


def first_kernel(spaces, base, groups, *refs):
    counts_ref, slots_ref, edge_slots_ref = refs[:3]
    parts, refs = refs[3 : 3 + spaces], refs[3 + spaces :]
    overs, refs = refs[: spaces - base], refs[spaces - base :]
    shares, refs = refs[:groups], refs[groups:]
    side_ref, weights_in, velocity_in = refs[:3]
    warped_ref, slopes_ref, scale_ref, field_ref, keep_ref, send_ref = refs[3:9]
    table, update, weights_ref, packs, chunk_sems = refs[9:]
    _, subj_dev, rows, plane, depth = weights_ref.shape
    total = parts[0].shape[0]
    short = parts[-1].shape[0] - 2 * EDGE
    cap = total - 2 * EDGE * subj_dev
    me, position = lax.axis_index("space"), lax.axis_index("subj")
    core = lax.bitwise_and(position, 1)
    odd = lax.bitwise_and(me, 1)
    chunks = chunk_sems.shape[0] // 2
    chunk = rows // chunks
    chunk_copies = []
    for i in range(chunks):
        part = pl.ds(i * chunk, chunk)
        chunk_copies.append(
            [
                pltpu.make_async_copy(source.at[:, :, part], target, chunk_sems.at[n])
                for n, source, target in (
                    (2 * i, weights_in, weights_ref.at[:, :, part]),
                    (2 * i + 1, velocity_in, field_ref.at[:, :, pl.ds(1 + i * chunk, chunk)]),
                )
            ]
        )
    for copy in sum(chunk_copies, []):
        copy.start()
    for k in range(spaces):
        for c in range(total):
            if k < base or c < short:
                table[k * total + c] = parts[k][c]
            else:
                table[k * total + c] = overs[k - base][c - short]
    for i in range(side_ref.shape[0]):
        packs[1 - odd, 2 * EDGE + i] = parts[1][total + 2 * EDGE + i]
        packs[odd, 2 * EDGE + i] = side_ref[i]
    for i in range(2 * EDGE):
        packs[1 - odd, i] = parts[1][total + i]
        packs[odd, i] = jnp.zeros_like(side_ref[0])
    other = lax.bitwise_xor(me, me - 1 + 2 * odd)
    for k in carries(spaces):

        @pl.when(other == k)
        def _(k=k):
            for i in range(2 * EDGE):
                packs[odd, i] = parts[k][(short if k >= base else total) + i]

    before_ref, after_ref = packs.at[0], packs.at[1]
    masks, halves = inside((plane, depth), 1.0), inside((plane, depth), 0.5)

    def tile(s, e, brick, fractions, live, f, current):
        w = warp_tile(brick.astype(jnp.float32), fractions, masks, live)
        g = slopes(w, halves)
        scale = 0.0625 / (g[0] * g[0] + g[1] * g[1] + g[2] * g[2] + RIDGE)
        ratio = (predict(w, g, f) - current) * scale
        warped_ref[s, e] = w
        scale_ref[s, e] = scale
        for c in range(3):
            slopes_ref[c, s, e] = g[c]
            update[c, s, e] = g[c] * ratio

    def row(r, carry):
        current = whole_row(shares, r, position)
        for s in range(subj_dev):
            count = counts_ref[0, s]
            first = lax.shift_right_logical(count, 1)
            alive = (r < first) | (r >= rows - (count - first))
            live = jnp.where(alive, 1.0, 0.0).astype(jnp.float32)
            wanted = slots_ref[s, r]
            owner = lax.div(wanted, cap)
            slot = lax.bitwise_xor(owner, me) * total + (wanted - owner * cap)
            tile(
                s,
                r + EDGE,
                table[slot],
                [weights_ref[c, s, r] for c in range(3)],
                live,
                [field_ref[c, s, r + 1] for c in range(3)],
                current,
            )
        return carry

    for side, (ref, there, e0) in enumerate(
        ((before_ref, me > 0, 0), (after_ref, me < spaces - 1, rows + EDGE))
    ):
        live = jnp.where(there, 1.0, 0.0).astype(jnp.float32)
        for r in range(EDGE):
            current = ref[2 * r].astype(jnp.float32) + ref[2 * r + 1].astype(jnp.float32)
            for s in range(subj_dev):
                at = [2 * ((c * subj_dev + s + 1) * EDGE + r) for c in range(3)]
                tile(
                    s,
                    e0 + r,
                    table[edge_slots_ref[(side * subj_dev + s) * EDGE + r]],
                    [ref[a + 1] for a in at],
                    live,
                    [ref[a].astype(jnp.float32) for a in at],
                    current,
                )

    for i in range(chunks):
        for copy in chunk_copies[i]:
            copy.wait()
        lax.fori_loop(i * chunk, (i + 1) * chunk, row, 0, unroll=8)

    for c in range(3):
        for s in range(subj_dev):
            at = 2 * (c * subj_dev + s + 1) * EDGE
            field_ref[c, s, 0] = before_ref[at + 2 * (EDGE - 1)].astype(jnp.float32)
            field_ref[c, s, rows + 1] = after_ref[at].astype(jnp.float32)

    def move(i, carry):
        e = i + EDGE - 1
        total_p = None
        for s in range(subj_dev):
            g = [slopes_ref[c, s, e] for c in range(3)]
            f = []
            for c in range(3):
                delta = smooth(update[c, s, e - 1], update[c, s, e], update[c, s, e + 1], masks)
                f.append(field_ref[c, s, i] - delta)
                field_ref[c, s, i] = f[c]
            p = predict(warped_ref[s, e], g, f)
            total_p = p if total_p is None else total_p + p
        half = plane // 2
        low, high = total_p[:half], total_p[half:]
        keep_ref[i] = jnp.where(core == 0, low, high)
        send_ref[i] = jnp.where(core == 0, high, low).astype(send_ref.dtype)
        return carry

    lax.fori_loop(0, rows + 2, move, 0, unroll=22)


def first(counts, slots, edge_slots, parts, overs, shares, side, weights, velocity):
    _, subj_dev, rows, plane, depth = velocity.shape
    spaces = len(parts)
    total = parts[0].shape[0]
    long = rows + 2 * EDGE
    sums = shaped((rows + 2, plane // 2, depth))
    arrays = [*parts, *overs, *shares, side]
    return pl.pallas_call(
        functools.partial(first_kernel, spaces, spaces - len(overs), len(shares)),
        out_shape=(
            shaped((subj_dev, long, plane, depth)),
            shaped((3, subj_dev, long, plane, depth)),
            shaped((subj_dev, long, plane, depth)),
            shaped((3, subj_dev, rows + 2, plane, depth)),
            sums,
            shaped(sums.shape, jnp.bfloat16),
        ),
        in_specs=[SMEM] * 3 + [VMEM] * len(arrays) + [ANY] * 2,
        out_specs=(VMEM,) * 6,
        scratch_shapes=[
            pltpu.VMEM((spaces * total, plane, depth), weights.dtype),
            pltpu.VMEM((3, subj_dev, long, plane, depth), jnp.float32),
            pltpu.VMEM(weights.shape, weights.dtype),
            pltpu.VMEM((2, side.shape[0] + 2 * EDGE) + side.shape[1:], side.dtype),
            pltpu.SemaphoreType.DMA((16,)),
        ],
        compiler_params=params(),
        name="first",
    )(counts, slots, edge_slots, *arrays, in_hbm(weights), in_hbm(velocity))


def last_kernel(
    mine_ref,
    other_ref,
    warped_ref,
    slopes_ref,
    scale_ref,
    field_ref,
    out_ref,
    keep_ref,
    send_ref,
    update,
    out,
    sems,
):
    _, subj_dev, rows, plane, depth = out.shape
    core = lax.bitwise_and(lax.axis_index("subj"), 1)
    masks = inside((plane, depth), 1.0)
    chunks = sems.shape[0]
    chunk = rows // chunks

    def renew(i, carry):
        mine, other = mine_ref[i].astype(jnp.float32), other_ref[i].astype(jnp.float32)
        current = jnp.concatenate(
            [jnp.where(core == 0, mine, other), jnp.where(core == 0, other, mine)], axis=0
        )
        for s in range(subj_dev):
            g = [slopes_ref[c, s, i + 1] for c in range(3)]
            f = [field_ref[c, s, i] for c in range(3)]
            ratio = (predict(warped_ref[s, i + 1], g, f) - current) * scale_ref[s, i + 1]
            for c in range(3):
                update[c, s, i] = g[c] * ratio
        return carry

    lax.fori_loop(0, rows + 2, renew, 0, unroll=22)

    def move(r, carry):
        total = None
        for s in range(subj_dev):
            g = [slopes_ref[c, s, r + EDGE] for c in range(3)]
            f = []
            for c in range(3):
                delta = smooth(update[c, s, r], update[c, s, r + 1], update[c, s, r + 2], masks)
                f.append(field_ref[c, s, r + 1] - delta)
                out[c, s, r] = f[c]
            p = predict(warped_ref[s, r + EDGE], g, f)
            total = p if total is None else total + p
        quarter = plane // 4
        low, high = total[: 2 * quarter], total[2 * quarter :]
        upper = lax.broadcasted_iota(jnp.int32, low.shape, 0) >= quarter
        even = jnp.where(upper, pltpu.roll(high, quarter, 0), low)
        odd = jnp.where(upper, high, pltpu.roll(low, quarter, 0))
        keep_ref[r] = jnp.where(core == 0, even, odd)
        send_ref[r] = jnp.where(core == 0, odd, even)
        return carry

    copies = []
    for i in range(chunks):
        lax.fori_loop(i * chunk, (i + 1) * chunk, move, 0, unroll=8)
        part = pl.ds(i * chunk, chunk)
        copy = pltpu.make_async_copy(out.at[:, :, part], out_ref.at[:, :, part], sems.at[i])
        copy.start()
        copies.append(copy)
    for copy in copies:
        copy.wait()


def last(mine, other, warped, slopes_all, scale, field, rows):
    _, subj_dev, _, plane, depth = field.shape
    shape = (3, subj_dev, rows, plane, depth)
    sums = shaped((rows, plane // 2, depth))
    return pl.pallas_call(
        last_kernel,
        out_shape=(shaped(shape), sums, sums),
        in_specs=[VMEM] * 6,
        out_specs=(ANY, VMEM, VMEM),
        scratch_shapes=[
            pltpu.VMEM(field.shape, jnp.float32),
            pltpu.VMEM(shape, jnp.float32),
            pltpu.SemaphoreType.DMA((8,)),
        ],
        compiler_params=params(),
        name="last",
    )(mine, other, warped, slopes_all, scale, field)


def fold_kernel(keep_ref, got_ref, own_ref, away_ref):
    second = lax.shift_right_logical(lax.axis_index("subj"), 1) == 1
    quarter = own_ref.shape[1]

    def row(r, carry):
        total = keep_ref[r] + got_ref[r]
        low, high = total[:quarter], total[quarter:]
        own_ref[r] = jnp.where(second, high, low)
        away_ref[r] = jnp.where(second, low, high)
        return carry

    lax.fori_loop(0, keep_ref.shape[0], row, 0, unroll=8)


def fold(keep, got):
    rows, half, depth = keep.shape
    part = shaped((rows, half // 2, depth))
    return pl.pallas_call(
        fold_kernel,
        out_shape=(part, part),
        in_specs=[VMEM] * 2,
        out_specs=(VMEM,) * 2,
        compiler_params=params(),
        name="fold",
    )(keep, got)


def swap(value, axis, mask):
    count = lax.axis_size(axis)
    return lax.ppermute(value, axis, [(i, i ^ mask) for i in range(count)])


def body(images, velocity, weights, template, owners, local_rows, tile_counts):
    spaces = lax.axis_size("space")
    groups = lax.axis_size("subj")
    subj_dev, rows, plane, depth = images.shape
    cap = subj_dev * (2 * rows // spaces)
    subjects = subj_dev * groups
    counts = jnp.swapaxes(tile_counts, 0, 1)

    request, slots, held, near_pack, side = plan(
        counts,
        jnp.swapaxes(owners, 1, 2),
        local_rows,
        images.reshape(subj_dev * rows, plane, depth),
        velocity,
        weights,
        cap,
        spaces,
    )
    others = [(i, i + 1) for i in range(1, spaces - 1, 2)]
    side = lax.ppermute(side, "space", others + [(j, i) for i, j in others])
    shares = [template] + [swap(template, "subj", k) for k in range(1, groups)]
    wanted = lax.all_to_all(request, "space", split_axis=0, concat_axis=0, tiled=True)

    base = spaces // 2
    total = cap + 2 * EDGE * subj_dev
    short = cap - cap // 8
    sizes = [total] * base + [short] * (spaces - base)
    sends, overs, edge_slots, over = pick(wanted, held, near_pack, shares, side, cap, sizes)
    far = [swap(sends[k], "space", k) for k in range(base, spaces)]
    near = [sends[0]] + [swap(sends[k], "space", k) for k in range(1, base)]

    def again(state):
        parts = [swap(part, "space", base + i) for i, part in enumerate(state[1])]
        return jnp.int32(0), parts

    _, overs = lax.while_loop(lambda state: state[0] > 0, again, (over[0], list(overs)))

    warped, slopes_all, scale, field, keep, send = first(
        counts, slots, edge_slots, near + far, overs, shares, side, weights, velocity
    )
    share = keep + swap(send, "subj", 1).astype(jnp.float32)
    mask = 2
    while mask < groups:
        share = share + swap(share.astype(jnp.bfloat16), "subj", mask).astype(jnp.float32)
        mask = 2 * mask
    mine = (share / subjects).astype(jnp.bfloat16)
    other = swap(mine, "subj", 1)

    field, keep, send = last(mine, other, warped, slopes_all, scale, field, rows)
    if groups == 4:
        own, away = fold(keep, swap(send, "subj", 1))
        result = (own + swap(away, "subj", 2)) / subjects
    else:
        quarter = plane // 4
        core = lax.bitwise_and(lax.axis_index("subj"), 1)
        even = jnp.where(core == 0, keep, send)
        odd = jnp.where(core == 0, send, keep)
        full = jnp.concatenate(
            [even[:, :quarter], odd[:, :quarter], even[:, quarter:], odd[:, quarter:]], axis=1
        )
        result = lax.psum_scatter(full, "subj", scatter_dimension=1, tiled=True) / subjects
    return field, result


def solution(mesh):
    in_specs = (
        P("subj", "space", None, None),
        P(None, "subj", "space", None, None),
        P(None, "subj", "space", None, None),
        P("space", "subj", None),
        P("subj", "space", None),
        P("subj", "space"),
        P("subj", "space"),
    )
    out_specs = (P(None, "subj", "space", None, None), P("space", "subj", None))
    return jax.shard_map(body, mesh=mesh, in_specs=in_specs, out_specs=out_specs, check_vma=False)
```
